256 devices in a mesh: row: 32 (over x, y, core), col: 8 (over z).
Axes of the slice: x: 4, y: 4, z: 8, core: 2. Of those that a mesh axis runs over, the one named last changes fastest.
Arguments:
- lower_earlier: bfloat16 [16, 96, 512, 512], P('col', 'row'), may hold values from -0.0546875 to 0.0546875
- lower_current: bfloat16 [16, 3, 512, 512], P('col', None, 'row'), may hold values from -0.25 to 0.25
- inverse_diagonal: bfloat16 [3, 512, 512], replicated, may hold values from -1 to 2, as said below
- solved_earlier: bfloat16 [96, 512, 1024], P('row'), may hold values from -6 to 6
- statistics: float32 [512, 16, 1024], P('row', 'col'), may hold values from -6 to 6
Outputs:
- reduced_statistics: float32 [512, 16, 1024], P('row', 'col')
- solved_blocks: bfloat16 [3, 512, 1024], P(None, 'row')
The draws below stay inside these ranges and needn't reach their ends.
Inputs may be any that keep to these rules, and one draw needn't show every extreme that they name: `inverse_diagonal`: each block is lower triangular with diagonal entries between 0.5 and 2 and entries below the diagonal of magnitude under one.
All inputs are finite; a program needn't handle non-finite values.
Results may differ from the reference program's by a relative error of at most 0.008.
Values may be sent and summed in bfloat16 or wider, within the bound.
A program may use at most 64 MiB of HBM per device.

```python
import math
import jax
import jax.numpy as jnp
from jax import lax

BLOCK = 512
STEPS = 3
OWN_ROWS = 2
EXPERIMENTS = 1024
TARGETS = 16
EARLIER = 96
N_COL = 8


def draw_inverse_diagonal(key, part):
    key = jax.random.fold_in(key, 7)
    first_key, second_key = jax.random.split(key)
    position = jnp.arange(BLOCK)
    below = (position[:, None] > position[None, :]).astype(jnp.float32)
    entries = jnp.clip(jax.random.normal(first_key, (STEPS, BLOCK, BLOCK), jnp.float32), -4.0, 4.0)
    diagonal = 0.5 * 4.0 ** jax.random.uniform(second_key, (STEPS, BLOCK), jnp.float32)
    spread_factor = 1.0 / math.sqrt(BLOCK)
    identity = jnp.eye(BLOCK, dtype=jnp.float32)[None]
    return (entries * below * spread_factor + diagonal[:, :, None] * identity).astype(jnp.bfloat16)


def strengthened(values, stream_key, source, target, parts, factor):
    owner, partner = [(jnp.arange(values.shape[dim]) // (values.shape[dim] // parts)).reshape([-1 if axis == dim else 1 for axis in range(values.ndim)]) for dim in (source, target)]
    chosen = jax.random.permutation(stream_key, parts)[partner]
    strong = (owner == chosen) | (owner == (partner + parts // 2) % parts)
    return jnp.where(strong, factor * values, values)


def levels(stream_key, extent, shards, smallest, top_value):
    def one(dim, shards_of):
        steps = jax.random.uniform(jax.random.fold_in(jax.random.fold_in(stream_key, 6), dim), (shards_of,), jnp.float32, smallest / len(shards), top_value / len(shards))
        return jnp.repeat(jnp.exp(steps), extent[dim] // shards_of).reshape((-1,) + (1,) * (len(extent) - dim - 1))

    factor_of = one(*shards[0])
    for cut in shards[1:]:
        factor_of = factor_of * one(*cut)
    return factor_of


def bell_draw(own_key, dims, spread, bound, shards=(), kind=jnp.bfloat16):
    values = spread * jax.random.normal(own_key, dims, jnp.float32)
    if shards:
        values = values * levels(own_key, dims, shards, -0.22, 0.18)
    return jnp.clip(values, -bound, bound).astype(kind)


def gaussian_with(key, shape, width, reach, shards, heavy, kind=jnp.bfloat16):
    values = width * jax.random.normal(key, shape, jnp.float32)
    if shards:
        values = values * levels(key, shape, shards, -0.22, 0.18)
    return jnp.clip(strengthened(values, jax.random.fold_in(key, 3), *heavy), -reach, reach).astype(kind)


def setup_inputs(seed: int = 0) -> dict:
    seeds = jax.random.split(jax.random.key(seed), 6)
    lower_earlier = gaussian_with(seeds[0], (TARGETS, EARLIER, BLOCK, BLOCK), (BLOCK * EARLIER) ** -0.5, 0.0546875, ((0, 8), (1, 32)), (1, 2, 32, 2.75))
    lower_current = bell_draw(seeds[1], (TARGETS, STEPS, BLOCK, BLOCK), BLOCK ** -0.5, 0.25, ((0, 8), (2, 32)))
    inverse_diagonal = draw_inverse_diagonal(jax.random.fold_in(seeds[5], 71), 0)
    solved_earlier = bell_draw(seeds[3], (EARLIER, BLOCK, EXPERIMENTS), 1.0, 6.0, ((0, 32),))
    statistics = bell_draw(seeds[4], (BLOCK, TARGETS, EXPERIMENTS), 1.0, 6.0, ((0, 32), (1, 8)), jnp.float32)
    return {"lower_earlier": lower_earlier, "lower_current": lower_current, "inverse_diagonal": inverse_diagonal, "solved_earlier": solved_earlier, "statistics": statistics}


def reference(lower_earlier, lower_current, inverse_diagonal, solved_earlier, statistics):
    widened = solved_earlier.astype(jnp.float32)

    def row_product(block_rows):
        return jnp.einsum("bnq,bqm->nm", block_rows.astype(jnp.float32), widened)

    earlier_sum = jnp.transpose(lax.map(row_product, lower_earlier), (1, 0, 2))
    reduced = statistics - earlier_sum
    solved = []
    for k in range(STEPS):
        leading = reduced[:, k * OWN_ROWS, :]
        for j in range(k):
            leading = leading - jnp.dot(lower_current[k * OWN_ROWS, j], solved[j], preferred_element_type=jnp.float32)
        pivotal = leading.astype(jnp.bfloat16)
        solved.append(jnp.dot(inverse_diagonal[k], pivotal, preferred_element_type=jnp.float32).astype(jnp.bfloat16))
    blocks = jnp.arange(TARGETS, dtype=jnp.int32)
    position = blocks // OWN_ROWS + N_COL * (blocks % OWN_ROWS)
    updated = reduced
    for k in range(STEPS):
        product = jnp.einsum("anq,qm->nam", lower_current[:, k].astype(jnp.float32), solved[k].astype(jnp.float32))
        active = (position > k)[None, :, None]
        updated = updated - jnp.where(active, product, jnp.float32(0.0))
    return updated, jnp.stack(solved)
```

```python
import jax
import jax.numpy as jnp
from jax import lax
from jax.experimental import pallas as pl
from jax.experimental.pallas import tpu as pltpu
from jax.sharding import PartitionSpec as P

MESH = pl.DeviceIdType.MESH
F32 = jnp.float32
BF16 = jnp.bfloat16
SIDE = 4
CHIPS = 16
PLANES = 8


def lanes_low(shape):
    return lax.broadcasted_iota(jnp.int32, shape, len(shape) - 1) < 64


def swap(value):
    return pltpu.roll(value, 64, 1)


def dot(a, b):
    return jnp.dot(a, b, preferred_element_type=F32)


def wait_bytes(ref, sem):
    pltpu.make_async_copy(ref, ref, sem).wait()


def kernel(
    le, s, lc, inv, stat, upd, sol,
    sv, lev, invv, statv, csend, crecv, acc, rssend, rsrecv, lg, stage, rz, q, xs, xg, usend, ug, red,
    load_sem, own_sem, c_ssem, c_rsem, rs_ssem, rs_rsem, l_ssem, l_rsem, st_ssem, st_rsem,
    rz_ssem, rz_rsem, z_ssem, z_rsem, q_ssem, q_rsem, x_ssem, x_rsem, u_ssem, u_rsem,
):
    row = lax.axis_index("row")
    z = lax.axis_index("col")
    c = lax.rem(row, 2)
    p = row // 2
    x = p // SIDE
    y = lax.rem(p, SIDE)
    sib = (row + 1 - 2 * c, z)
    low = lanes_low((128, 128))

    def peer(d):
        px = lax.rem(x + d // SIDE, SIDE)
        py = lax.rem(y + lax.rem(d, SIDE), SIDE)
        return px * SIDE + py

    def remote(src, dst, ssem, rsem, device):
        return pltpu.make_async_remote_copy(
            src_ref=src, dst_ref=dst, send_sem=ssem, recv_sem=rsem, device_id=device, device_id_type=MESH
        )

    loads = []
    for a, slot in ((0, 0), (0, 1), (1, 0), (1, 1)):
        half = (1 - c) if slot == 0 else c
        loads.append(pltpu.make_async_copy(le.at[a, :, :, half], lev.at[a, slot], load_sem.at[2 * a + slot]))
    s_loads = [pltpu.make_async_copy(s.at[b], sv.at[b], load_sem.at[4 + b]) for b in range(3)]
    inv_load = pltpu.make_async_copy(inv, invv, load_sem.at[7])
    stat_load = pltpu.make_async_copy(stat, statv, load_sem.at[8])
    loads[0].start()
    for cp in s_loads:
        cp.start()
    for cp in loads[1:] + [stat_load, inv_load]:
        cp.start()

    barrier = pltpu.get_barrier_semaphore()

    def greet(d, carry):
        pl.semaphore_signal(barrier, inc=1, device_id=(2 * peer(d) + c, z), device_id_type=MESH)
        return carry

    def greet_z(d, carry):
        pl.semaphore_signal(barrier, inc=1, device_id=(row, lax.rem(z + d, PLANES)), device_id_type=MESH)
        return carry

    pl.semaphore_signal(barrier, inc=1, device_id=sib, device_id_type=MESH)
    lax.fori_loop(1, CHIPS, greet, 0)
    lax.fori_loop(1, PLANES, greet_z, 0)

    def product(a, slot, columns):
        total = None
        for b in range(3):
            term = dot(lev[a, slot, b].reshape(256, 512), sv[b, :, columns])
            total = term if total is None else total + term
        return total

    def block_columns(i):
        return pl.ds(pl.multiple_of(lax.rem(x + i, SIDE) * 256, 256), 256)

    def c_copy(a, i):
        return remote(csend.at[a, i], crecv.at[a, i], c_ssem.at[a, i], c_rsem.at[a, i], sib)

    def other_block(a, i):
        csend[a, i] = product(a, 0, block_columns(i)).astype(BF16)

    def own_block(a, i):
        columns = block_columns(i)
        total = product(a, 1, columns)
        c_copy(a, i).wait_recv()
        acc[...] = total + crecv[a, i].astype(F32)
        mine = pl.ds(pl.multiple_of(16 * p, 16), 16)
        acc[mine, :] = acc[mine, :] - statv[:, a, columns]
        for t in range(2):
            lo = acc[0:128, 128 * t : 128 * t + 128]
            hi = acc[128:256, 128 * t : 128 * t + 128]
            rssend[a, SIDE * i + 2 * t] = jnp.where(low, lo, swap(hi)).astype(BF16)
            rssend[a, SIDE * i + 2 * t + 1] = jnp.where(low, swap(lo), hi).astype(BF16)

        def send(j):
            py = lax.rem(y + j, SIDE)
            px = lax.rem(x + i, SIDE)
            remote(
                rssend.at[a, SIDE * i + py],
                rsrecv.at[a, SIDE * i + j],
                rs_ssem.at[a],
                rs_rsem.at[a],
                (2 * (px * SIDE + py) + c, z),
            ).start()

        for j in range(SIDE):
            if j == 0:
                pl.when(i > 0)(lambda: send(0))
            else:
                send(j)

    def both_halves(a, first):
        def other(i, carry):
            other_block(a, i)
            c_copy(a, i).start()
            return carry

        def own(i, carry):
            own_block(a, i)
            return carry

        lax.fori_loop(first, SIDE, other, 0)
        loads[2 * a + 1].wait()
        lax.fori_loop(0, SIDE, own, 0)

    loads[0].wait()
    for cp in s_loads:
        cp.wait()
    other_block(0, 0)
    pl.semaphore_wait(barrier, CHIPS - 1 + 1 + PLANES - 1)
    c_copy(0, 0).start()

    stage_copies = (
        remote(lc.at[0, pl.ds(0, 1)], stage.at[pl.ds(0, 1)], st_ssem, st_rsem.at[0], (row, 0)),
        remote(lc.at[0, pl.ds(0, 2)], stage.at[pl.ds(1, 2)], st_ssem, st_rsem.at[1], (row, 0)),
    )
    for t in range(2):
        pl.when(z == t + 1)(lambda: stage_copies[t].start())
    stat_load.wait()
    both_halves(0, 1)

    def gather(part, src):
        def send(d, carry):
            remote(
                src, lg.at[pl.ds(3 * part, 3), p], l_ssem.at[part], l_rsem.at[part], (2 * peer(d) + c, z)
            ).start()
            return carry

        lax.fori_loop(1, CHIPS, send, 0)
        pltpu.make_async_copy(src, lg.at[pl.ds(3 * part, 3), p], own_sem.at[part]).start()

    def gather_wait(part):
        wait_bytes(lg.at[pl.ds(3 * part, 3), pl.ds(0, CHIPS - 1)], l_rsem.at[part])
        wait_bytes(stage, own_sem.at[part])

    @pl.when(z != 0)
    def _():
        gather(0, lc.at[0])

    @pl.when(z == 0)
    def _():
        for t in range(2):
            stage_copies[t].wait_recv()
        gather(0, stage)

    gather(1, lc.at[1])

    loads[2].wait()
    both_halves(1, 0)
    inv_load.wait()

    def reduced(a):
        wait_bytes(rsrecv.at[a, pl.ds(1, CHIPS - 1)], rs_rsem.at[a])
        total = rssend[a, y].astype(F32)
        for d in range(1, CHIPS):
            total = total + rsrecv[a, d].astype(F32)
        red[a] = -total

    reduced(0)

    rz[2] = red[0]
    rz_copies = [remote(rz.at[2], rz.at[t], rz_ssem, rz_rsem.at[t], (row, 0)) for t in range(2)]
    for t in range(2):
        pl.when(z == t + 1)(lambda: rz_copies[t].start())

    def applied(block, k):
        panel = lg[block].reshape(256, 512)
        solved = xs[k].reshape(256, 128)
        first = dot(panel[:, 0:256], solved)
        second = dot(panel[:, 256:512], solved)
        return jnp.where(low, first[0:128], second[128:256]) + swap(
            jnp.where(low, first[128:256], second[0:128])
        )

    def update(k):
        red[1] = red[1] - applied(3 + k, k)

        @pl.when(z > k)
        def _():
            red[0] = red[0] - applied(k, k)

    def x_send(k):
        def send(d, carry):
            target = peer(d)
            remote(
                xs.at[k, lax.rem(target, 8), c], xg.at[k, p], x_ssem.at[k], x_rsem.at[k], (2 * target + c, z)
            ).start()
            return carry

        lax.fori_loop(1, CHIPS, send, 0)
        xg[k, p] = xs[k, lax.rem(p, 8), c]

    def z_copy(k, d):
        return remote(
            q.at[k, :, c], q.at[k, :, c], z_ssem.at[k, d - 1], z_rsem.at[k], (row, lax.rem(z + d, PLANES))
        )

    def sib_copy(k):
        return remote(q.at[k, :, c], q.at[k, :, c], q_ssem.at[k], q_rsem.at[k], sib)

    def sib_back(k):
        return remote(q.at[k, :, 1 - c], q.at[k, :, 1 - c], q_ssem.at[k], q_rsem.at[k], sib)

    for k in range(3):

        @pl.when(z == 0)
        def _():
            if k == 0:
                pivotal = red[0]
            elif k == 1:
                gather_wait(0)
                pivotal = -applied(0, 0)
                rz_copies[0].wait_recv()
                pivotal = rz[0] + pivotal
            else:
                pivotal = -applied(1, 0) - applied(2, 1)
                rz_copies[1].wait_recv()
                pivotal = rz[1] + pivotal
            q[k, :, c] = pivotal.astype(BF16).reshape(8, 16, 128)
            sib_copy(k).start()
            for d in range(1, PLANES):
                z_copy(k, d).start()

        @pl.when(z != 0)
        def _():
            if k == 1:
                gather_wait(0)
                gather_wait(1)
                reduced(1)
            if k > 0:
                x_send(k - 1)
                update(k - 1)
            z_copy(k, 1).wait_recv()
            sib_copy(k).start()

        sib_back(k).wait_recv()
        pivotal = q[k].reshape(256, 128)
        left = dot(invv[k, :, 0:256], pivotal)
        right = dot(invv[k, 256:512, 256:512], pivotal)
        low_x = lanes_low((256, 128))
        solved = jnp.where(low_x, left[0:256], right + swap(left[256:512]))
        xs[k] = solved.astype(BF16).reshape(8, 2, 16, 128)

    @pl.when(z == 0)
    def _():
        gather_wait(1)
        reduced(1)
        for k in range(2):
            x_send(k)
            update(k)

    @pl.when((z == 1) | (z == 2))
    def _():
        wait_bytes(rz.at[2], rz_ssem)

    update(2)
    first, second = red[0], red[1]
    usend[0:8] = jnp.where(low, first, swap(second)).reshape(8, 16, 128)
    usend[8:16] = jnp.where(low, swap(first), second).reshape(8, 16, 128)

    def u_send(d, carry):
        target = peer(d)
        remote(usend.at[target], ug.at[p], u_ssem, u_rsem, (2 * target + c, z)).start()
        return carry

    lax.fori_loop(1, CHIPS, u_send, 0)
    ug[p] = usend[p]
    x_send(2)

    low_t = lanes_low((16, 128))
    early = p < 8

    def solved_out(k):
        wait_bytes(xg.at[k, pl.ds(0, CHIPS - 1)], x_rsem.at[k])
        for t in range(8):
            even = xg[k, 2 * t].astype(F32)
            odd = xg[k, 2 * t + 1].astype(F32)
            value = jnp.where(
                early, jnp.where(low_t, even, swap(odd)), jnp.where(low_t, swap(even), odd)
            )
            sol[k, :, 128 * t : 128 * t + 128] = value.astype(BF16)

    solved_out(0)
    solved_out(1)
    wait_bytes(ug.at[pl.ds(0, CHIPS - 1)], u_rsem)
    for t in range(8):
        even, odd = ug[2 * t], ug[2 * t + 1]
        upd[0, :, 128 * t : 128 * t + 128] = jnp.where(low_t, even, swap(odd))
        upd[1, :, 128 * t : 128 * t + 128] = jnp.where(low_t, swap(even), odd)
    solved_out(2)

    for a in range(2):
        for i in range(SIDE):
            c_copy(a, i).wait_send()
        wait_bytes(rssend.at[a, pl.ds(0, CHIPS - 1)], rs_ssem.at[a])
        wait_bytes(lg.at[pl.ds(3 * a, 3), pl.ds(0, CHIPS - 1)], l_ssem.at[a])
    for t in range(2):
        pl.when(z == t + 1)(lambda: stage_copies[t].wait_send())
    for k in range(3):
        sib_copy(k).wait_send()
        wait_bytes(xg.at[k, pl.ds(0, CHIPS - 1)], x_ssem.at[k])

        @pl.when(z == 0)
        def _():
            for d in range(1, PLANES):
                z_copy(k, d).wait_send()

    wait_bytes(ug.at[pl.ds(0, CHIPS - 1)], u_ssem)


def per_device(lower_earlier, lower_current, inverse_diagonal, solved_earlier, statistics):
    dma = pltpu.SemaphoreType.DMA
    any_space = pl.BlockSpec(memory_space=pl.ANY)
    vmem = pl.BlockSpec(memory_space=pltpu.VMEM)
    upd, sol = pl.pallas_call(
        kernel,
        out_shape=(
            jax.ShapeDtypeStruct((2, 16, 1024), F32),
            jax.ShapeDtypeStruct((3, 16, 1024), BF16),
        ),
        in_specs=[any_space] * 5,
        out_specs=(vmem, vmem),
        scratch_shapes=[
            pltpu.VMEM((3, 512, 1024), BF16),
            pltpu.VMEM((2, 2, 3, 16, 16, 512), BF16),
            pltpu.VMEM((3, 512, 512), BF16),
            pltpu.VMEM((16, 2, 1024), F32),
            pltpu.VMEM((2, 4, 256, 256), BF16),
            pltpu.VMEM((2, 4, 256, 256), BF16),
            pltpu.VMEM((256, 256), F32),
            pltpu.VMEM((2, 16, 128, 128), BF16),
            pltpu.VMEM((2, 16, 128, 128), BF16),
            pltpu.VMEM((6, 16, 16, 512), BF16),
            pltpu.VMEM((3, 16, 512), BF16),
            pltpu.VMEM((3, 128, 128), F32),
            pltpu.VMEM((3, 8, 2, 16, 128), BF16),
            pltpu.VMEM((3, 8, 2, 16, 128), BF16),
            pltpu.VMEM((3, 16, 16, 128), BF16),
            pltpu.VMEM((16, 16, 128), F32),
            pltpu.VMEM((16, 16, 128), F32),
            pltpu.VMEM((2, 128, 128), F32),
            dma((9,)),
            dma((2,)),
            dma((2, 4)), dma((2, 4)),
            dma((2,)), dma((2,)),
            dma((2,)), dma((2,)),
            dma, dma((2,)),
            dma, dma((2,)),
            dma((3, 7)), dma((3,)),
            dma((3,)), dma((3,)),
            dma((3,)), dma((3,)),
            dma, dma,
        ],
        compiler_params=pltpu.CompilerParams(
            collective_id=0, has_side_effects=True, vmem_limit_bytes=56 * 1024 * 1024
        ),
        cost_estimate=pl.CostEstimate(flops=3400000000, bytes_accessed=9000000, transcendentals=0),
    )(
        lower_earlier.reshape(2, 3, 16, 2, 16, 512),
        solved_earlier,
        lower_current,
        inverse_diagonal,
        statistics,
    )
    return jnp.swapaxes(upd, 0, 1), sol


def solution(mesh):
    placed = (
        P("col", "row", None, None),
        P("col", None, "row", None),
        P(),
        P("row", None, None),
        P("row", "col", None),
    )
    return jax.shard_map(
        per_device,
        mesh=mesh,
        in_specs=placed,
        out_specs=(P("row", "col", None), P(None, "row", None)),
        check_vma=False,
    )
```

```python
import jax
import jax.numpy as jnp
from jax import lax
from jax.experimental import pallas as pl
from jax.experimental.pallas import tpu as pltpu
from jax.sharding import PartitionSpec as P

MESH = pl.DeviceIdType.MESH
F32 = jnp.float32
BF16 = jnp.bfloat16
SIDE = 4
CHIPS = 16
PLANES = 8


def lanes_low(shape):
    return lax.broadcasted_iota(jnp.int32, shape, len(shape) - 1) < 64


def swap(value):
    return pltpu.roll(value, 64, 1)


def dot(a, b):
    return jnp.dot(a, b, preferred_element_type=F32)


def wait_bytes(ref, sem):
    pltpu.make_async_copy(ref, ref, sem).wait()


def kernel(
    le, s, lc, inv, stat, upd, sol,
    sv, lev, invv, statv, csend, crecv, acc, rssend, rsrecv, lg, rz, q, xs, xg, usend, ug, red,
    load_sem, own_sem, c_ssem, c_rsem, rs_ssem, rs_rsem, l_ssem, l_rsem, f_ssem, f_rsem, ch_ssem,
    rz_ssem, rz_rsem, z_ssem, z_rsem, q_ssem, q_rsem, x_ssem, x_rsem, u_ssem, u_rsem,
):
    row = lax.axis_index("row")
    z = lax.axis_index("col")
    c = lax.rem(row, 2)
    p = row // 2
    x = p // SIDE
    y = lax.rem(p, SIDE)
    sib = (row + 1 - 2 * c, z)
    low = lanes_low((128, 128))

    def peer(d):
        px = lax.rem(x + d // SIDE, SIDE)
        py = lax.rem(y + lax.rem(d, SIDE), SIDE)
        return px * SIDE + py

    def x_peer(d):
        return 2 * (lax.rem(x + d, SIDE) * SIDE + y) + c

    def y_peer(d):
        return 2 * (x * SIDE + lax.rem(y + d, SIDE)) + c

    def remote(src, dst, ssem, rsem, device):
        return pltpu.make_async_remote_copy(
            src_ref=src, dst_ref=dst, send_sem=ssem, recv_sem=rsem, device_id=device, device_id_type=MESH
        )

    loads = []
    for a, slot in ((0, 0), (0, 1), (1, 0), (1, 1)):
        half = (1 - c) if slot == 0 else c
        loads.append(pltpu.make_async_copy(le.at[a, :, :, half], lev.at[a, slot], load_sem.at[2 * a + slot]))
    s_loads = [pltpu.make_async_copy(s.at[b], sv.at[b], load_sem.at[4 + b]) for b in range(3)]
    inv_load = pltpu.make_async_copy(inv, invv, load_sem.at[7])
    stat_load = pltpu.make_async_copy(stat, statv, load_sem.at[8])
    loads[0].start()
    for cp in s_loads:
        cp.start()
    for cp in loads[1:] + [stat_load, inv_load]:
        cp.start()

    barrier = pltpu.get_barrier_semaphore()

    def greet(d, carry):
        pl.semaphore_signal(barrier, inc=1, device_id=(2 * peer(d) + c, z), device_id_type=MESH)
        return carry

    pl.semaphore_signal(barrier, inc=1, device_id=sib, device_id_type=MESH)
    lax.fori_loop(1, CHIPS, greet, 0)

    @pl.when(z == 0)
    def _():
        for d in range(1, PLANES):
            pl.semaphore_signal(barrier, inc=1, device_id=(row, d), device_id_type=MESH)
        for t in range(1, 3):
            for d in range(1, SIDE):
                pl.semaphore_signal(barrier, inc=1, device_id=(x_peer(d), t), device_id_type=MESH)

    @pl.when(z > 0)
    def _():
        pl.semaphore_signal(barrier, inc=1, device_id=(row, 0), device_id_type=MESH)

    @pl.when((z == 1) | (z == 2))
    def _():
        for d in range(1, SIDE):
            pl.semaphore_signal(barrier, inc=1, device_id=(x_peer(d), 0), device_id_type=MESH)

    partners = CHIPS + jnp.where(z == 0, 7 + 6, jnp.where(z <= 2, 1 + 3, 1))

    def product(a, slot, columns):
        total = None
        for b in range(3):
            term = dot(lev[a, slot, b].reshape(256, 512), sv[b, :, columns])
            total = term if total is None else total + term
        return total

    def block_columns(i):
        return pl.ds(pl.multiple_of(lax.rem(x + i, SIDE) * 256, 256), 256)

    def c_copy(a, i):
        return remote(csend.at[a, i], crecv.at[a, i], c_ssem.at[a, i], c_rsem.at[a, i], sib)

    def other_block(a, i):
        csend[a, i] = product(a, 0, block_columns(i)).astype(BF16)

    def own_block(a, i):
        columns = block_columns(i)
        total = product(a, 1, columns)
        c_copy(a, i).wait_recv()
        acc[...] = total + crecv[a, i].astype(F32)
        mine = pl.ds(pl.multiple_of(16 * p, 16), 16)
        acc[mine, :] = acc[mine, :] - statv[:, a, columns]
        for t in range(2):
            lo = acc[0:128, 128 * t : 128 * t + 128]
            hi = acc[128:256, 128 * t : 128 * t + 128]
            rssend[a, SIDE * i + 2 * t] = jnp.where(low, lo, swap(hi)).astype(BF16)
            rssend[a, SIDE * i + 2 * t + 1] = jnp.where(low, swap(lo), hi).astype(BF16)

        def send(j):
            py = lax.rem(y + j, SIDE)
            px = lax.rem(x + i, SIDE)
            remote(
                rssend.at[a, SIDE * i + py],
                rsrecv.at[a, SIDE * i + j],
                rs_ssem.at[a],
                rs_rsem.at[a],
                (2 * (px * SIDE + py) + c, z),
            ).start()

        for j in range(SIDE):
            if j == 0:
                pl.when(i > 0)(lambda: send(0))
            else:
                send(j)

    def both_halves(a, first, between=None):
        def other(i, carry):
            other_block(a, i)
            c_copy(a, i).start()
            return carry

        def own(i, carry):
            own_block(a, i)
            return carry

        lax.fori_loop(first, SIDE, other, 0)
        if between is not None:
            between()
        loads[2 * a + 1].wait()
        lax.fori_loop(0, SIDE, own, 0)

    loads[0].wait()
    for cp in s_loads:
        cp.wait()
    other_block(0, 0)
    pl.semaphore_wait(barrier, partners)
    c_copy(0, 0).start()

    def near(part, device):
        remote(lc.at[part], lg.at[pl.ds(3 * part, 3), x, y], l_ssem.at[part], l_rsem.at[part], device).start()

    own_part = [pltpu.make_async_copy(lc.at[t], lg.at[pl.ds(3 * t, 3), x, y], own_sem.at[t]) for t in range(2)]

    def chain_block(t, d):
        span = pl.ds(t - 1, t)
        return remote(
            lc.at[0, pl.ds(0, t)], lg.at[span, x, y], ch_ssem.at[d], l_rsem.at[0], (x_peer(d), 0)
        )

    @pl.when(z != 0)
    def _():
        for d in range(1, SIDE):
            near(0, (x_peer(d), z))
        own_part[0].start()

    for t in (1, 2):

        @pl.when(z == t)
        def _():
            for d in range(SIDE):
                chain_block(t, d).start()

    for d in range(1, SIDE):
        near(1, (y_peer(d), z))
    own_part[1].start()

    stat_load.wait()
    both_halves(0, 1)

    def far_source(part):
        return lg.at[pl.ds(0, 3), :, y] if part == 0 else lg.at[pl.ds(3, 3), x]

    def far(part):
        for d in range(1, SIDE):
            device = (y_peer(d) if part == 0 else x_peer(d), z)
            remote(far_source(part), far_source(part), f_ssem.at[part], f_rsem.at[part], device).start()

    def three_near(part):
        return lg.at[pl.ds(3 * part, 3), 0, pl.ds(0, 3)]

    def three_far(part):
        return lg.at[pl.ds(3 * part, 3), pl.ds(0, 3)]

    def near_wait(part):
        wait_bytes(three_near(part), l_rsem.at[part])
        own_part[part].wait()

    def gather_wait(part):
        wait_bytes(three_far(part), f_rsem.at[part])

    def relay():
        @pl.when(z != 0)
        def _():
            near_wait(0)
            far(0)

        near_wait(1)
        far(1)

    loads[2].wait()
    both_halves(1, 0, relay)

    @pl.when(z == 0)
    def _():
        wait_bytes(far_source(0), l_rsem.at[0])
        far(0)

    inv_load.wait()

    def reduced(a):
        wait_bytes(rsrecv.at[a, pl.ds(1, CHIPS - 1)], rs_rsem.at[a])
        total = rssend[a, y].astype(F32)
        for d in range(1, CHIPS):
            total = total + rsrecv[a, d].astype(F32)
        red[a] = -total

    reduced(0)

    rz[2] = red[0]
    rz_copies = [remote(rz.at[2], rz.at[t], rz_ssem, rz_rsem.at[t], (row, 0)) for t in range(2)]
    for t in range(2):
        pl.when(z == t + 1)(lambda: rz_copies[t].start())

    def applied(block, k):
        panel = lg[block].reshape(256, 512)
        solved = xs[k].reshape(256, 128)
        first = dot(panel[:, 0:256], solved)
        second = dot(panel[:, 256:512], solved)
        return jnp.where(low, first[0:128], second[128:256]) + swap(
            jnp.where(low, first[128:256], second[0:128])
        )

    def update(k):
        red[1] = red[1] - applied(3 + k, k)

        @pl.when(z > k)
        def _():
            red[0] = red[0] - applied(k, k)

    def x_send(k):
        def send(d, carry):
            target = peer(d)
            remote(
                xs.at[k, lax.rem(target, 8), c], xg.at[k, p], x_ssem.at[k], x_rsem.at[k], (2 * target + c, z)
            ).start()
            return carry

        lax.fori_loop(1, CHIPS, send, 0)
        xg[k, p] = xs[k, lax.rem(p, 8), c]

    def z_copy(k, d):
        return remote(
            q.at[k, :, c], q.at[k, :, c], z_ssem.at[k, d - 1], z_rsem.at[k], (row, lax.rem(z + d, PLANES))
        )

    def sib_copy(k):
        return remote(q.at[k, :, c], q.at[k, :, c], q_ssem.at[k], q_rsem.at[k], sib)

    def sib_back(k):
        return remote(q.at[k, :, 1 - c], q.at[k, :, 1 - c], q_ssem.at[k], q_rsem.at[k], sib)

    for k in range(3):

        @pl.when(z == 0)
        def _():
            if k == 0:
                pivotal = red[0]
            elif k == 1:
                gather_wait(0)
                pivotal = -applied(0, 0)
                rz_copies[0].wait_recv()
                pivotal = rz[0] + pivotal
            else:
                pivotal = -applied(1, 0) - applied(2, 1)
                rz_copies[1].wait_recv()
                pivotal = rz[1] + pivotal
            q[k, :, c] = pivotal.astype(BF16).reshape(8, 16, 128)
            sib_copy(k).start()
            for d in range(1, PLANES):
                z_copy(k, d).start()

        @pl.when(z != 0)
        def _():
            if k == 1:
                gather_wait(0)
                gather_wait(1)
                reduced(1)
            if k > 0:
                x_send(k - 1)
                update(k - 1)
            z_copy(k, 1).wait_recv()
            sib_copy(k).start()

        sib_back(k).wait_recv()
        pivotal = q[k].reshape(256, 128)
        left = dot(invv[k, :, 0:256], pivotal)
        right = dot(invv[k, 256:512, 256:512], pivotal)
        low_x = lanes_low((256, 128))
        solved = jnp.where(low_x, left[0:256], right + swap(left[256:512]))
        xs[k] = solved.astype(BF16).reshape(8, 2, 16, 128)

    @pl.when(z == 0)
    def _():
        gather_wait(1)
        reduced(1)
        for k in range(2):
            x_send(k)
            update(k)

    @pl.when((z == 1) | (z == 2))
    def _():
        wait_bytes(rz.at[2], rz_ssem)

    update(2)
    first, second = red[0], red[1]
    usend[0:8] = jnp.where(low, first, swap(second)).reshape(8, 16, 128)
    usend[8:16] = jnp.where(low, swap(first), second).reshape(8, 16, 128)

    def u_send(d, carry):
        target = peer(d)
        remote(usend.at[target], ug.at[p], u_ssem, u_rsem, (2 * target + c, z)).start()
        return carry

    lax.fori_loop(1, CHIPS, u_send, 0)
    ug[p] = usend[p]
    x_send(2)

    low_t = lanes_low((16, 128))
    early = p < 8

    def solved_out(k):
        wait_bytes(xg.at[k, pl.ds(0, CHIPS - 1)], x_rsem.at[k])
        for t in range(8):
            even = xg[k, 2 * t].astype(F32)
            odd = xg[k, 2 * t + 1].astype(F32)
            value = jnp.where(
                early, jnp.where(low_t, even, swap(odd)), jnp.where(low_t, swap(even), odd)
            )
            sol[k, :, 128 * t : 128 * t + 128] = value.astype(BF16)

    solved_out(0)
    solved_out(1)
    wait_bytes(ug.at[pl.ds(0, CHIPS - 1)], u_rsem)
    for t in range(8):
        even, odd = ug[2 * t], ug[2 * t + 1]
        upd[0, :, 128 * t : 128 * t + 128] = jnp.where(low_t, even, swap(odd))
        upd[1, :, 128 * t : 128 * t + 128] = jnp.where(low_t, swap(even), odd)
    solved_out(2)

    for a in range(2):
        for i in range(SIDE):
            c_copy(a, i).wait_send()
        wait_bytes(rssend.at[a, pl.ds(0, CHIPS - 1)], rs_ssem.at[a])
        wait_bytes(three_far(a), f_ssem.at[a])

    @pl.when(z != 0)
    def _():
        wait_bytes(three_near(0), l_ssem.at[0])

    wait_bytes(three_near(1), l_ssem.at[1])
    for t in (1, 2):

        @pl.when(z == t)
        def _():
            for d in range(SIDE):
                chain_block(t, d).wait_send()

    for k in range(3):
        sib_copy(k).wait_send()
        wait_bytes(xg.at[k, pl.ds(0, CHIPS - 1)], x_ssem.at[k])

        @pl.when(z == 0)
        def _():
            for d in range(1, PLANES):
                z_copy(k, d).wait_send()

    wait_bytes(ug.at[pl.ds(0, CHIPS - 1)], u_ssem)


def per_device(lower_earlier, lower_current, inverse_diagonal, solved_earlier, statistics):
    dma = pltpu.SemaphoreType.DMA
    any_space = pl.BlockSpec(memory_space=pl.ANY)
    vmem = pl.BlockSpec(memory_space=pltpu.VMEM)
    upd, sol = pl.pallas_call(
        kernel,
        out_shape=(
            jax.ShapeDtypeStruct((2, 16, 1024), F32),
            jax.ShapeDtypeStruct((3, 16, 1024), BF16),
        ),
        in_specs=[any_space] * 5,
        out_specs=(vmem, vmem),
        scratch_shapes=[
            pltpu.VMEM((3, 512, 1024), BF16),
            pltpu.VMEM((2, 2, 3, 16, 16, 512), BF16),
            pltpu.VMEM((3, 512, 512), BF16),
            pltpu.VMEM((16, 2, 1024), F32),
            pltpu.VMEM((2, 4, 256, 256), BF16),
            pltpu.VMEM((2, 4, 256, 256), BF16),
            pltpu.VMEM((256, 256), F32),
            pltpu.VMEM((2, 16, 128, 128), BF16),
            pltpu.VMEM((2, 16, 128, 128), BF16),
            pltpu.VMEM((6, 4, 4, 16, 512), BF16),
            pltpu.VMEM((3, 128, 128), F32),
            pltpu.VMEM((3, 8, 2, 16, 128), BF16),
            pltpu.VMEM((3, 8, 2, 16, 128), BF16),
            pltpu.VMEM((3, 16, 16, 128), BF16),
            pltpu.VMEM((16, 16, 128), F32),
            pltpu.VMEM((16, 16, 128), F32),
            pltpu.VMEM((2, 128, 128), F32),
            dma((9,)),
            dma((2,)),
            dma((2, 4)), dma((2, 4)),
            dma((2,)), dma((2,)),
            dma((2,)), dma((2,)),
            dma((2,)), dma((2,)),
            dma((4,)),
            dma, dma((2,)),
            dma((3, 7)), dma((3,)),
            dma((3,)), dma((3,)),
            dma((3,)), dma((3,)),
            dma, dma,
        ],
        compiler_params=pltpu.CompilerParams(
            collective_id=0, has_side_effects=True, vmem_limit_bytes=56 * 1024 * 1024
        ),
        cost_estimate=pl.CostEstimate(flops=3400000000, bytes_accessed=9000000, transcendentals=0),
    )(
        lower_earlier.reshape(2, 3, 16, 2, 16, 512),
        solved_earlier,
        lower_current,
        inverse_diagonal,
        statistics,
    )
    return jnp.swapaxes(upd, 0, 1), sol


def solution(mesh):
    placed = (
        P("col", "row", None, None),
        P("col", None, "row", None),
        P(),
        P("row", None, None),
        P("row", "col", None),
    )
    return jax.shard_map(
        per_device,
        mesh=mesh,
        in_specs=placed,
        out_specs=(P("row", "col", None), P(None, "row", None)),
        check_vma=False,
    )
```

```python
import jax
import jax.numpy as jnp
from jax import lax
from jax.experimental import pallas as pl
from jax.experimental.pallas import tpu as pltpu
from jax.sharding import PartitionSpec as P

MESH = pl.DeviceIdType.MESH
F32 = jnp.float32
BF16 = jnp.bfloat16
SIDE = 4
CHIPS = 16
PLANES = 8


def lanes_low(shape):
    return lax.broadcasted_iota(jnp.int32, shape, len(shape) - 1) < 64


def swap(value):
    return pltpu.roll(value, 64, 1)


def dot(a, b):
    return jnp.dot(a, b, preferred_element_type=F32)


def wait_bytes(ref, sem):
    pltpu.make_async_copy(ref, ref, sem).wait()


def kernel(
    le, s, lc, inv, stat, upd, sol,
    sv, lev, invv, statv, csend, crecv, acc, rssend, rsrecv, lg, rz, q, xs, xg, usend, ug, red,
    load_sem, own_sem, c_ssem, c_rsem, rs_ssem, rs_rsem, l_ssem, l_rsem, f_ssem, f_rsem, ch_ssem, ch_rsem, ready_sem,
    rz_ssem, rz_rsem, z_ssem, z_rsem, q_ssem, q_rsem, x_ssem, x_rsem, u_ssem, u_rsem,
):
    row = lax.axis_index("row")
    z = lax.axis_index("col")
    c = lax.rem(row, 2)
    p = row // 2
    x = p // SIDE
    y = lax.rem(p, SIDE)
    sib = (row + 1 - 2 * c, z)
    low = lanes_low((128, 128))

    def peer(d):
        px = lax.rem(x + d // SIDE, SIDE)
        py = lax.rem(y + lax.rem(d, SIDE), SIDE)
        return px * SIDE + py

    def x_peer(d):
        return 2 * (lax.rem(x + d, SIDE) * SIDE + y) + c

    def y_peer(d):
        return 2 * (x * SIDE + lax.rem(y + d, SIDE)) + c

    def remote(src, dst, ssem, rsem, device):
        return pltpu.make_async_remote_copy(
            src_ref=src, dst_ref=dst, send_sem=ssem, recv_sem=rsem, device_id=device, device_id_type=MESH
        )

    loads = []
    for a, slot in ((0, 0), (0, 1), (1, 0), (1, 1)):
        half = (1 - c) if slot == 0 else c
        loads.append(pltpu.make_async_copy(le.at[a, :, :, half], lev.at[a, slot], load_sem.at[2 * a + slot]))
    s_loads = [pltpu.make_async_copy(s.at[b], sv.at[b], load_sem.at[4 + b]) for b in range(3)]
    inv_load = pltpu.make_async_copy(inv, invv, load_sem.at[7])
    stat_load = pltpu.make_async_copy(stat, statv, load_sem.at[8])
    loads[0].start()
    for cp in s_loads:
        cp.start()
    for cp in loads[1:] + [stat_load, inv_load]:
        cp.start()

    barrier = pltpu.get_barrier_semaphore()

    def greet(d, carry):
        pl.semaphore_signal(barrier, inc=1, device_id=(2 * peer(d) + c, z), device_id_type=MESH)
        return carry

    def signal(sem, device):
        pl.semaphore_signal(sem, inc=1, device_id=device, device_id_type=MESH)

    @pl.when(z == 0)
    def _():
        for d in (4, 3, 5, 6, 7, 2, 1):
            signal(barrier, (row, d))
        for t in (2, 1):
            for d in (2, 1, 3):
                signal(barrier, (x_peer(d), t))
                signal(barrier, (y_peer(d), t))

    @pl.when((z == 1) | (z == 2))
    def _():
        signal(barrier, (row, 0))
        for d in (2, 1, 3):
            signal(barrier, (x_peer(d), 0))
            signal(barrier, (y_peer(d), 0))

    lax.fori_loop(1, CHIPS, greet, 0)
    signal(barrier, sib)
    partners = CHIPS + jnp.where(z == 0, 2 * 7, jnp.where(z <= 2, 7, 1))

    def product(a, slot, columns):
        total = None
        for b in range(3):
            term = dot(lev[a, slot, b].reshape(256, 512), sv[b, :, columns])
            total = term if total is None else total + term
        return total

    def block_columns(i):
        return pl.ds(pl.multiple_of(lax.rem(x + i, SIDE) * 256, 256), 256)

    def nth(t):
        return lax.rem(t + 2, SIDE)

    def c_copy(a, i):
        return remote(csend.at[a, i], crecv.at[a, i], c_ssem.at[a, i], c_rsem.at[a, i], sib)

    def other_block(a, i):
        csend[a, i] = product(a, 0, block_columns(nth(i))).astype(BF16)

    def own_block(a, turn):
        i = nth(turn)
        columns = block_columns(i)
        total = product(a, 1, columns)
        c_copy(a, turn).wait_recv()
        acc[...] = total + crecv[a, turn].astype(F32)
        mine = pl.ds(pl.multiple_of(16 * p, 16), 16)
        acc[mine, :] = acc[mine, :] - statv[:, a, columns]
        for t in range(2):
            lo = acc[0:128, 128 * t : 128 * t + 128]
            hi = acc[128:256, 128 * t : 128 * t + 128]
            rssend[a, SIDE * i + 2 * t] = jnp.where(low, lo, swap(hi)).astype(BF16)
            rssend[a, SIDE * i + 2 * t + 1] = jnp.where(low, swap(lo), hi).astype(BF16)

        def send(j):
            py = lax.rem(y + j, SIDE)
            px = lax.rem(x + i, SIDE)
            remote(
                rssend.at[a, SIDE * i + py],
                rsrecv.at[a, SIDE * i + j],
                rs_ssem.at[a],
                rs_rsem.at[a],
                (2 * (px * SIDE + py) + c, z),
            ).start()

        for j in (2, 1, 3, 0):
            if j == 0:
                pl.when(i > 0)(lambda: send(0))
            else:
                send(j)

    def both_halves(a, first, between=None):
        def other(i, carry):
            other_block(a, i)
            c_copy(a, i).start()
            return carry

        def own(i, carry):
            own_block(a, i)
            return carry

        lax.fori_loop(first, SIDE, other, 0)
        if between is not None:
            between()
        loads[2 * a + 1].wait()
        lax.fori_loop(0, SIDE, own, 0)

    loads[0].wait()
    for cp in s_loads:
        cp.wait()
    other_block(0, 0)
    pl.semaphore_wait(barrier, partners)
    c_copy(0, 0).start()

    pl.when(z > 2)(lambda: signal(ready_sem, (row, 0)))

    halves = (pl.ds(0, 256), pl.ds(256, 256))

    def along(h, d):
        return y_peer(d) if h else x_peer(d)

    def near(part, count):
        for d in (2, 1, 3):
            for h in range(2):
                remote(
                    lc.at[part, pl.ds(0, count), :, halves[h]],
                    lg.at[pl.ds(3 * part, count), x, y, :, halves[h]],
                    l_ssem.at[part, h],
                    l_rsem.at[part, h],
                    (along(h, d), z),
                ).start()

    own_part = [pltpu.make_async_copy(lc.at[t], lg.at[pl.ds(3 * t, 3), x, y], own_sem.at[t]) for t in range(2)]

    def chain_near(t, h, d):
        return remote(
            lc.at[0, pl.ds(0, t), :, halves[h]],
            lg.at[pl.ds(t - 1, t), x, y, :, halves[h]],
            ch_ssem.at[h, d],
            ch_rsem.at[t - 1, h],
            (along(h, d), 0),
        )

    for t in (1, 2):

        @pl.when(z == t)
        def _():
            for d in range(SIDE):
                for h in range(2):
                    chain_near(t, h, d).start()
            near(0, t)

    pl.when(z > 2)(lambda: near(0, 3))
    pl.when(z > 0)(lambda: own_part[0].start())
    near(1, 3)
    own_part[1].start()

    stat_load.wait()
    both_halves(0, 1)

    def source(first, count, h):
        span = pl.ds(first, count)
        return lg.at[span, x, :, :, halves[h]] if h else lg.at[span, :, y, :, halves[h]]

    def far(first, count, sem):
        for h in range(2):
            for d in (2, 1, 3):
                device = (along(1 - h, d), z)
                remote(
                    source(first, count, h), source(first, count, h), f_ssem.at[sem, h], f_rsem.at[sem, h], device
                ).start()

    def three_near(first, count, h):
        return lg.at[pl.ds(first, count), 0, pl.ds(0, 3), :, halves[h]]

    def three_far(first, count, h):
        return lg.at[pl.ds(first, count), pl.ds(0, 3), :, :, halves[h]]

    def relay_chain(t):
        for h in range(2):
            wait_bytes(source(t - 1, t, h), ch_rsem.at[t - 1, h])
        far(t - 1, t, 2 * t - 2)

    def relay(part, count):
        own_part[part].wait()
        for h in range(2):
            wait_bytes(three_near(3 * part, count, h), l_rsem.at[part, h])
        far(3 * part, count, part)

    def gather_wait(first, count, sem):
        for h in range(2):
            wait_bytes(three_far(first, count, h), f_rsem.at[sem, h])

    @pl.when(z == 0)
    def _():
        relay_chain(1)
        relay_chain(2)

    def between():
        @pl.when(z > 2)
        def _():
            relay(0, 3)
            relay(1, 3)

    loads[2].wait()
    both_halves(1, 0, between)
    inv_load.wait()

    def reduced(a):
        wait_bytes(rsrecv.at[a, pl.ds(1, CHIPS - 1)], rs_rsem.at[a])
        total = rssend[a, y].astype(F32)
        for d in range(1, CHIPS):
            total = total + rsrecv[a, d].astype(F32)
        red[a] = -total

    reduced(0)

    rz[2] = red[0]
    rz_copies = [remote(rz.at[2], rz.at[t], rz_ssem, rz_rsem.at[t], (row, 0)) for t in range(2)]
    for t in (1, 2):

        @pl.when(z == t)
        def _():
            rz_copies[t - 1].start()
            relay(0, t)
            relay(1, 3)


    def applied(block, k):
        panel = lg[block].reshape(256, 512)
        solved = xs[k].reshape(256, 128)
        first = dot(panel[:, 0:256], solved)
        second = dot(panel[:, 256:512], solved)
        return jnp.where(low, first[0:128], second[128:256]) + swap(
            jnp.where(low, first[128:256], second[0:128])
        )

    def update(k):
        red[1] = red[1] - applied(3 + k, k)

        @pl.when(z > k)
        def _():
            red[0] = red[0] - applied(k, k)

    def x_send(k):
        def send(d, carry):
            target = peer(d)
            remote(
                xs.at[k, lax.rem(target, 8), c], xg.at[k, p], x_ssem.at[k], x_rsem.at[k], (2 * target + c, z)
            ).start()
            return carry

        lax.fori_loop(1, CHIPS, send, 0)
        xg[k, p] = xs[k, lax.rem(p, 8), c]

    def z_copy(k, d):
        return remote(
            q.at[k, :, c], q.at[k, :, c], z_ssem.at[k, d - 1], z_rsem.at[k], (row, lax.rem(z + d, PLANES))
        )

    def sib_copy(k):
        return remote(q.at[k, :, c], q.at[k, :, c], q_ssem.at[k], q_rsem.at[k], sib)

    def sib_back(k):
        return remote(q.at[k, :, 1 - c], q.at[k, :, 1 - c], q_ssem.at[k], q_rsem.at[k], sib)

    for k in range(3):

        @pl.when(z == 0)
        def _():
            if k == 0:
                pivotal = red[0]
            elif k == 1:
                gather_wait(0, 1, 0)
                pivotal = -applied(0, 0)
                rz_copies[0].wait_recv()
                pivotal = rz[0] + pivotal
            else:
                gather_wait(1, 2, 2)
                pivotal = -applied(1, 0) - applied(2, 1)
                rz_copies[1].wait_recv()
                pivotal = rz[1] + pivotal
            q[k, :, c] = pivotal.astype(BF16).reshape(8, 16, 128)
            sib_copy(k).start()
            if k == 0:
                pl.semaphore_wait(ready_sem, PLANES - 3)
            for d in range(1, PLANES):
                z_copy(k, d).start()
            if k == 0:
                relay(1, 3)

        @pl.when(z != 0)
        def _():
            if k == 1:
                for t in (1, 2):
                    pl.when(z == t)(lambda: gather_wait(0, t, 0))
                pl.when(z > 2)(lambda: gather_wait(0, 3, 0))
                gather_wait(3, 3, 1)
                reduced(1)
            if k > 0:
                x_send(k - 1)
                update(k - 1)
            z_copy(k, 1).wait_recv()
            sib_copy(k).start()

        sib_back(k).wait_recv()
        pivotal = q[k].reshape(256, 128)
        left = dot(invv[k, :, 0:256], pivotal)
        right = dot(invv[k, 256:512, 256:512], pivotal)
        low_x = lanes_low((256, 128))
        solved = jnp.where(low_x, left[0:256], right + swap(left[256:512]))
        xs[k] = solved.astype(BF16).reshape(8, 2, 16, 128)

    @pl.when(z == 0)
    def _():
        reduced(1)
        gather_wait(3, 3, 1)
        for k in range(2):
            x_send(k)
            update(k)

    @pl.when((z == 1) | (z == 2))
    def _():
        wait_bytes(rz.at[2], rz_ssem)

    update(2)
    first, second = red[0], red[1]
    usend[0:8] = jnp.where(low, first, swap(second)).reshape(8, 16, 128)
    usend[8:16] = jnp.where(low, swap(first), second).reshape(8, 16, 128)

    def u_send(d, carry):
        target = peer(d)
        remote(usend.at[target], ug.at[p], u_ssem, u_rsem, (2 * target + c, z)).start()
        return carry

    lax.fori_loop(1, CHIPS, u_send, 0)
    ug[p] = usend[p]
    x_send(2)

    low_t = lanes_low((16, 128))
    early = p < 8

    def solved_out(k):
        wait_bytes(xg.at[k, pl.ds(0, CHIPS - 1)], x_rsem.at[k])
        for t in range(8):
            even = xg[k, 2 * t].astype(F32)
            odd = xg[k, 2 * t + 1].astype(F32)
            value = jnp.where(
                early, jnp.where(low_t, even, swap(odd)), jnp.where(low_t, swap(even), odd)
            )
            sol[k, :, 128 * t : 128 * t + 128] = value.astype(BF16)

    solved_out(0)
    solved_out(1)
    wait_bytes(ug.at[pl.ds(0, CHIPS - 1)], u_rsem)
    for t in range(8):
        even, odd = ug[2 * t], ug[2 * t + 1]
        upd[0, :, 128 * t : 128 * t + 128] = jnp.where(low_t, even, swap(odd))
        upd[1, :, 128 * t : 128 * t + 128] = jnp.where(low_t, swap(even), odd)
    solved_out(2)

    for a in range(2):
        for i in range(SIDE):
            c_copy(a, i).wait_send()
        wait_bytes(rssend.at[a, pl.ds(0, CHIPS - 1)], rs_ssem.at[a])

    def far_sent(first, count, sem):
        for h in range(2):
            wait_bytes(three_far(first, count, h), f_ssem.at[sem, h])

    def near_sent(part, count):
        for h in range(2):
            wait_bytes(three_near(3 * part, count, h), l_ssem.at[part, h])

    for t in (1, 2):

        @pl.when(z == t)
        def _():
            near_sent(0, t)
            far_sent(0, t, 0)
            for d in range(SIDE):
                for h in range(2):
                    chain_near(t, h, d).wait_send()

    @pl.when(z > 2)
    def _():
        near_sent(0, 3)
        far_sent(0, 3, 0)

    @pl.when(z == 0)
    def _():
        far_sent(0, 1, 0)
        far_sent(1, 2, 2)

    near_sent(1, 3)
    far_sent(3, 3, 1)
    for k in range(3):
        sib_copy(k).wait_send()
        wait_bytes(xg.at[k, pl.ds(0, CHIPS - 1)], x_ssem.at[k])

        @pl.when(z == 0)
        def _():
            for d in range(1, PLANES):
                z_copy(k, d).wait_send()

    wait_bytes(ug.at[pl.ds(0, CHIPS - 1)], u_ssem)


def per_device(lower_earlier, lower_current, inverse_diagonal, solved_earlier, statistics):
    dma = pltpu.SemaphoreType.DMA
    any_space = pl.BlockSpec(memory_space=pl.ANY)
    vmem = pl.BlockSpec(memory_space=pltpu.VMEM)
    upd, sol = pl.pallas_call(
        kernel,
        out_shape=(
            jax.ShapeDtypeStruct((2, 16, 1024), F32),
            jax.ShapeDtypeStruct((3, 16, 1024), BF16),
        ),
        in_specs=[any_space] * 5,
        out_specs=(vmem, vmem),
        scratch_shapes=[
            pltpu.VMEM((3, 512, 1024), BF16),
            pltpu.VMEM((2, 2, 3, 16, 16, 512), BF16),
            pltpu.VMEM((3, 512, 512), BF16),
            pltpu.VMEM((16, 2, 1024), F32),
            pltpu.VMEM((2, 4, 256, 256), BF16),
            pltpu.VMEM((2, 4, 256, 256), BF16),
            pltpu.VMEM((256, 256), F32),
            pltpu.VMEM((2, 16, 128, 128), BF16),
            pltpu.VMEM((2, 16, 128, 128), BF16),
            pltpu.VMEM((6, 4, 4, 16, 512), BF16),
            pltpu.VMEM((3, 128, 128), F32),
            pltpu.VMEM((3, 8, 2, 16, 128), BF16),
            pltpu.VMEM((3, 8, 2, 16, 128), BF16),
            pltpu.VMEM((3, 16, 16, 128), BF16),
            pltpu.VMEM((16, 16, 128), F32),
            pltpu.VMEM((16, 16, 128), F32),
            pltpu.VMEM((2, 128, 128), F32),
            dma((9,)),
            dma((2,)),
            dma((2, 4)), dma((2, 4)),
            dma((2,)), dma((2,)),
            dma((2, 2)), dma((2, 2)),
            dma((3, 2)), dma((3, 2)),
            dma((2, 4)), dma((2, 2)),
            pltpu.SemaphoreType.REGULAR,
            dma, dma((2,)),
            dma((3, 7)), dma((3,)),
            dma((3,)), dma((3,)),
            dma((3,)), dma((3,)),
            dma, dma,
        ],
        compiler_params=pltpu.CompilerParams(
            collective_id=0, has_side_effects=True, vmem_limit_bytes=56 * 1024 * 1024
        ),
        cost_estimate=pl.CostEstimate(flops=3400000000, bytes_accessed=9000000, transcendentals=0),
    )(
        lower_earlier.reshape(2, 3, 16, 2, 16, 512),
        solved_earlier,
        lower_current,
        inverse_diagonal,
        statistics,
    )
    return jnp.swapaxes(upd, 0, 1), sol


def solution(mesh):
    placed = (
        P("col", "row", None, None),
        P("col", None, "row", None),
        P(),
        P("row", None, None),
        P("row", "col", None),
    )
    return jax.shard_map(
        per_device,
        mesh=mesh,
        in_specs=placed,
        out_specs=(P("row", "col", None), P(None, "row", None)),
        check_vma=False,
    )
```

```python
import jax
import jax.numpy as jnp
from jax import lax
from jax.experimental import pallas as pl
from jax.experimental.pallas import tpu as pltpu
from jax.sharding import PartitionSpec as P

MESH = pl.DeviceIdType.MESH
F32 = jnp.float32
BF16 = jnp.bfloat16
SIDE = 4
CHIPS = 16
PLANES = 8


def lanes_low(shape):
    return lax.broadcasted_iota(jnp.int32, shape, len(shape) - 1) < 64


def swap(value):
    return pltpu.roll(value, 64, 1)


def dot(a, b):
    return jnp.dot(a, b, preferred_element_type=F32)


def wait_bytes(ref, sem):
    pltpu.make_async_copy(ref, ref, sem).wait()


def kernel(
    le, s, lc, inv, stat, ug, xg,
    sv, lev, invv, statv, csend, crecv, acc, rssend, rsrecv, mid, last, lg, rz, q, xs, usend, red,
    le_sem, load_sem, mine_sem, own_sem, c_ssem, c_rsem, rs_ssem, rs_rsem, l_ssem, l_rsem, f_ssem, f_rsem, ch_ssem, ch_rsem, ready_sem,
    r2_ssem, r2_rsem, rz_ssem, rz_rsem, z_ssem, z_rsem, q_ssem, q_rsem, x_ssem, x_rsem, u_ssem, u_rsem,
):
    row = lax.axis_index("row")
    z = lax.axis_index("col")
    c = lax.rem(row, 2)
    p = row // 2
    x = p // SIDE
    y = lax.rem(p, SIDE)
    sib = (row + 1 - 2 * c, z)
    low = lanes_low((128, 128))
    steps = (0, 1, 2, 1)
    by_distance = sorted(range(1, CHIPS), key=lambda d: -steps[d // SIDE] - steps[d % SIDE])

    def peer(d):
        px = lax.rem(x + d // SIDE, SIDE)
        py = lax.rem(y + lax.rem(d, SIDE), SIDE)
        return px * SIDE + py

    def x_peer(d):
        return 2 * (lax.rem(x + d, SIDE) * SIDE + y) + c

    def y_peer(d):
        return 2 * (x * SIDE + lax.rem(y + d, SIDE)) + c

    def remote(src, dst, ssem, rsem, device):
        return pltpu.make_async_remote_copy(
            src_ref=src, dst_ref=dst, send_sem=ssem, recv_sem=rsem, device_id=device, device_id_type=MESH
        )

    def block_columns(i):
        return pl.ds(pl.multiple_of(lax.rem(x + i, SIDE) * 256, 256), 256)

    def nth(t):
        return lax.rem(t + 2, SIDE)

    def le_load(a, slot, b):
        half = c if slot else 1 - c
        return pltpu.make_async_copy(
            le.at[a, b, :, half], lev.at[a, slot, :, :, pl.ds(512 * b, 512)], le_sem.at[a, slot, b]
        )

    def s_load(t):
        columns = block_columns(nth(t))
        return pltpu.make_async_copy(s.at[:, columns], sv.at[:, columns], load_sem.at[t])

    def le_loads(a):
        return [le_load(a, slot, b) for slot in range(2) for b in range(3)]

    inv_load = pltpu.make_async_copy(inv, invv, load_sem.at[4])
    stat_load = pltpu.make_async_copy(stat, statv, load_sem.at[5])
    for cp in le_loads(0) + [s_load(t) for t in range(SIDE)] + le_loads(1) + [stat_load, inv_load]:
        cp.start()

    barrier = pltpu.get_barrier_semaphore()

    def greet(d, carry):
        pl.semaphore_signal(barrier, inc=1, device_id=(2 * peer(d) + c, z), device_id_type=MESH)
        return carry

    def signal(sem, device):
        pl.semaphore_signal(sem, inc=1, device_id=device, device_id_type=MESH)

    @pl.when(z == 0)
    def _():
        for d in (4, 3, 5, 6, 7, 2, 1):
            signal(barrier, (row, d))
        for t in (2, 1):
            for d in (2, 1, 3):
                signal(barrier, (x_peer(d), t))
                signal(barrier, (y_peer(d), t))

    @pl.when((z == 1) | (z == 2))
    def _():
        signal(barrier, (row, 0))
        for d in (2, 1, 3):
            signal(barrier, (x_peer(d), 0))
            signal(barrier, (y_peer(d), 0))

    lax.fori_loop(1, CHIPS, greet, 0)
    signal(barrier, sib)
    partners = CHIPS + jnp.where(z == 0, 2 * 7, jnp.where(z <= 2, 7, 1))

    def c_copy(a, i):
        return remote(csend.at[a, i], crecv.at[a, i], c_ssem.at[a, i], c_rsem.at[a, i], sib)

    def multiply(a, t):
        if a == 0:
            s_load(t).wait()
        both = dot(lev[a].reshape(512, 1536), sv[:, block_columns(nth(t))])
        csend[a, t] = both[0:256].astype(BF16)
        acc[t] = both[256:512]

    def rs_send(a, i, j):
        py = lax.rem(y + j, SIDE)
        px = lax.rem(x + i, SIDE)
        remote(
            rssend.at[a, i, py],
            rsrecv.at[SIDE * i + j],
            rs_ssem.at[a, 0],
            rs_rsem.at[a, 0],
            (2 * (px * SIDE + py) + c, z),
        ).start()

    top, bottom = pl.ds(0, 64), pl.ds(64, 64)

    def first_x(a, i):
        remote(
            rssend.at[a, i, :, top],
            mid.at[a, 0, i],
            rs_ssem.at[a, 0],
            rs_rsem.at[a, 0],
            (2 * (lax.rem(x + i, SIDE) * SIDE + y) + c, z),
        ).start()

    def first_y(a):
        for j in (2, 1, 3):
            remote(
                rssend.at[a, :, lax.rem(y + j, SIDE), bottom],
                mid.at[a, 1, j],
                rs_ssem.at[a, 1],
                rs_rsem.at[a, 1],
                (y_peer(j), z),
            ).start()

    def rs_relay(a):
        wait_bytes(mid.at[a, 0, pl.ds(1, 3)], rs_rsem.at[a, 0])
        total = rssend[a, 0, :, 0:64].astype(F32)
        for d in range(1, SIDE):
            total = total + mid[a, 0, d].astype(F32)
        mid[a, 0, 0] = total.astype(BF16)
        for j in (2, 1, 3):
            remote(
                mid.at[a, 0, 0, lax.rem(y + j, SIDE)], last.at[a, 0, j], r2_ssem.at[a, 0], r2_rsem.at[a, 0], (y_peer(j), z)
            ).start()
        wait_bytes(mid.at[a, 1, pl.ds(1, 3)], rs_rsem.at[a, 1])
        total = rssend[a, :, y, 64:128].astype(F32)
        for d in range(1, SIDE):
            total = total + mid[a, 1, d].astype(F32)
        mid[a, 1, 0] = total.astype(BF16)
        for i in (2, 1, 3):
            remote(
                mid.at[a, 1, 0, i], last.at[a, 1, i], r2_ssem.at[a, 1], r2_rsem.at[a, 1], (x_peer(i), z)
            ).start()

    def rs_last(a):
        for h in range(2):
            wait_bytes(last.at[a, h, pl.ds(1, 3)], r2_rsem.at[a, h])
            total = mid[a, h, 0, (0 if h else y)].astype(F32)
            for d in range(1, SIDE):
                total = total + last[a, h, d].astype(F32)
            red[a, 64 * h : 64 * h + 64] = -total

    def rs_sent(a):
        for h in range(2):
            wait_bytes(mid.at[a, h, pl.ds(1, 3)], rs_ssem.at[a, h])
            wait_bytes(last.at[a, h, pl.ds(1, 3)], r2_ssem.at[a, h])

    def finish(a, turn):
        i = nth(turn)
        columns = block_columns(i)
        c_copy(a, turn).wait_recv()
        acc[turn] = acc[turn] + crecv[a, turn].astype(F32)
        mine = pl.ds(pl.multiple_of(16 * p, 16), 16)
        acc[turn, mine, :] = acc[turn, mine, :] - statv[:, a, columns]
        for t in range(2):
            lo = acc[turn, 0:128, 128 * t : 128 * t + 128]
            hi = acc[turn, 128:256, 128 * t : 128 * t + 128]
            rssend[a, i, 2 * t] = jnp.where(low, lo, swap(hi)).astype(BF16)
            rssend[a, i, 2 * t + 1] = jnp.where(low, swap(lo), hi).astype(BF16)

        def sends():
            for j in (2, 1, 3):
                rs_send(a, i, j)
            pl.when(i > 0)(lambda: rs_send(a, i, 0))

        if a == 0:
            pl.when(z <= 2)(sends)
            pl.when((z > 2) & (i > 0))(lambda: first_x(a, i))
        else:
            pl.when(i > 0)(lambda: first_x(a, i))

    def turns(a, first, last_turn):
        def turn(t, carry):
            @pl.when(t < SIDE)
            def _():
                multiply(a, t)
                c_copy(a, t).start()

            pl.when(t >= 2)(lambda: finish(a, t - 2))
            return carry

        lax.fori_loop(first, last_turn, turn, 0)

    for cp in le_loads(0):
        cp.wait()
    multiply(0, 0)
    pl.semaphore_wait(barrier, partners)
    c_copy(0, 0).start()

    pl.when(z > 2)(lambda: signal(ready_sem, (row, 0)))

    halves = (pl.ds(0, 256), pl.ds(256, 256))

    def along(h, d):
        return y_peer(d) if h else x_peer(d)

    def own_slot(part, h, span):
        return lg.at[part, 1, x, y, span] if h else lg.at[part, 0, y, x, span]

    def near(part, count):
        for d in (2, 1, 3):
            for h in range(2):
                remote(
                    lc.at[part, pl.ds(0, count), :, halves[h]],
                    own_slot(part, h, pl.ds(0, count)),
                    l_ssem.at[part, h],
                    l_rsem.at[part, h],
                    (along(h, d), z),
                ).start()

    own_part = [
        [
            pltpu.make_async_copy(lc.at[t, :, :, halves[h]], own_slot(t, h, pl.ds(0, 3)), own_sem.at[t, h])
            for h in range(2)
        ]
        for t in range(2)
    ]

    def own_start(part):
        for cp in own_part[part]:
            cp.start()

    def chain_near(t, h, d):
        return remote(
            lc.at[0, pl.ds(0, t), :, halves[h]],
            own_slot(0, h, pl.ds(t - 1, t)),
            ch_ssem.at[h, d],
            ch_rsem.at[t - 1, h],
            (along(h, d), 0),
        )

    for t in (1, 2):

        @pl.when(z == t)
        def _():
            for d in range(SIDE):
                for h in range(2):
                    chain_near(t, h, d).start()
            near(0, t)

    pl.when(z > 2)(lambda: near(0, 3))
    pl.when(z > 0)(lambda: own_start(0))
    near(1, 3)
    own_start(1)

    stat_load.wait()
    turns(0, 1, SIDE + 2)
    pl.when(z > 2)(lambda: first_y(0))

    def source(part, span, h):
        return lg.at[part, 1, x, :, span] if h else lg.at[part, 0, y, :, span]

    def far(part, span, sem):
        for h in range(2):
            for d in (2, 1, 3):
                device = (along(1 - h, d), z)
                remote(
                    source(part, span, h), source(part, span, h), f_ssem.at[sem, h], f_rsem.at[sem, h], device
                ).start()

    def three_near(part, span, h):
        return lg.at[part, h, 0, pl.ds(0, 3), span]

    def three_far(part, span, h):
        return lg.at[part, h, pl.ds(0, 3), :, span]

    def relay_chain(t):
        for h in range(2):
            wait_bytes(source(0, pl.ds(t - 1, t), h), ch_rsem.at[t - 1, h])
        far(0, pl.ds(t - 1, t), 2 * t - 2)

    def relay(part, count):
        for cp in own_part[part]:
            cp.wait()
        for h in range(2):
            wait_bytes(three_near(part, pl.ds(0, count), h), l_rsem.at[part, h])
        far(part, pl.ds(0, count), part)

    def gather_wait(part, span, sem):
        for h in range(2):
            wait_bytes(three_far(part, span, h), f_rsem.at[sem, h])

    @pl.when(z == 0)
    def _():
        relay_chain(1)
        relay_chain(2)

    def between():
        @pl.when(z > 2)
        def _():
            relay(0, 3)
            relay(1, 3)

    for cp in le_loads(1):
        cp.wait()
    turns(1, 0, 3)
    between()
    turns(1, 3, SIDE + 2)
    first_y(1)
    inv_load.wait()

    @pl.when(z <= 2)
    def _():
        wait_bytes(rsrecv.at[pl.ds(1, CHIPS - 1)], rs_rsem.at[0, 0])
        total = rssend[0, 0, y].astype(F32)
        for d in range(1, CHIPS):
            total = total + rsrecv[d].astype(F32)
        red[0] = -total

    @pl.when(z > 2)
    def _():
        rs_relay(0)
        rs_relay(1)
        rs_last(0)

    rz[2] = red[0]
    rz_copies = [remote(rz.at[2], rz.at[t], rz_ssem, rz_rsem.at[t], (row, 0)) for t in range(2)]
    for t in (1, 2):

        @pl.when(z == t)
        def _():
            rz_copies[t - 1].start()
            relay(0, t)
            relay(1, 3)
            rs_relay(1)


    def applied(block, k):
        part, slot = divmod(block, 3)
        solved = xs[k].reshape(256, 128)
        chips = [(i, j) for i in range(SIDE) for j in range(SIDE)]
        first = dot(jnp.concatenate([lg[part, 0, j, i, slot] for i, j in chips], axis=0), solved)
        second = dot(jnp.concatenate([lg[part, 1, i, j, slot] for i, j in chips], axis=0), solved)
        return jnp.where(low, first[0:128], second[128:256]) + swap(
            jnp.where(low, first[128:256], second[0:128])
        )

    def update(k):
        red[1] = red[1] - applied(3 + k, k)

        @pl.when(z > k)
        def _():
            red[0] = red[0] - applied(k, k)

    def own_x(k):
        return pltpu.make_async_copy(xs.at[k, lax.rem(p, 8), c], xg.at[k, p], mine_sem.at[k])

    def x_send(k):
        def send(d, carry):
            target = peer(d)
            remote(
                xs.at[k, lax.rem(target, 8), c], xg.at[k, p], x_ssem.at[k], x_rsem.at[k], (2 * target + c, z)
            ).start()
            return carry

        lax.fori_loop(1, CHIPS, send, 0)
        own_x(k).start()

    def z_copy(k, d):
        return remote(
            q.at[k, c], q.at[k, c], z_ssem.at[k, d - 1], z_rsem.at[k], (row, lax.rem(z + d, PLANES))
        )

    def sib_copy(k):
        return remote(q.at[k, c], q.at[k, c], q_ssem.at[k], q_rsem.at[k], sib)

    def sib_back(k):
        return remote(q.at[k, 1 - c], q.at[k, 1 - c], q_ssem.at[k], q_rsem.at[k], sib)

    for k in range(3):

        @pl.when(z == 0)
        def _():
            if k == 0:
                pivotal = red[0]
            elif k == 1:
                gather_wait(0, pl.ds(0, 1), 0)
                pivotal = -applied(0, 0)
                rz_copies[0].wait_recv()
                pivotal = rz[0] + pivotal
            else:
                gather_wait(0, pl.ds(1, 2), 2)
                pivotal = -applied(1, 0) - applied(2, 1)
                rz_copies[1].wait_recv()
                pivotal = rz[1] + pivotal
            q[k, c] = pivotal.astype(BF16).reshape(8, 16, 128)
            sib_copy(k).start()
            if k == 0:
                pl.semaphore_wait(ready_sem, PLANES - 3)
            for d in (4, 5, 3, 6, 2, 7, 1):
                z_copy(k, d).start()
            if k == 0:
                relay(1, 3)
                rs_relay(1)

        @pl.when(z != 0)
        def _():
            if k == 1:
                for t in (1, 2):
                    pl.when(z == t)(lambda: gather_wait(0, pl.ds(0, t), 0))
                pl.when(z > 2)(lambda: gather_wait(0, pl.ds(0, 3), 0))
                gather_wait(1, pl.ds(0, 3), 1)
                rs_last(1)
            if k > 0:
                x_send(k - 1)
                update(k - 1)
            z_copy(k, 1).wait_recv()
            sib_copy(k).start()

        sib_back(k).wait_recv()
        pivotal = jnp.concatenate([q[k, h, g] for g in range(8) for h in range(2)], axis=0)
        left = dot(invv[k, :, 0:256], pivotal)
        right = dot(invv[k, 256:512, 256:512], pivotal)
        low_x = lanes_low((256, 128))
        solved = jnp.where(low_x, left[0:256], right + swap(left[256:512]))
        xs[k] = solved.astype(BF16).reshape(8, 2, 16, 128)

    @pl.when(z == 0)
    def _():
        rs_last(1)
        gather_wait(1, pl.ds(0, 3), 1)
        for k in range(2):
            x_send(k)
            update(k)

    @pl.when((z == 1) | (z == 2))
    def _():
        wait_bytes(rz.at[2], rz_ssem)

    update(2)
    first, second = red[0], red[1]
    usend[0:8, 0:16] = jnp.where(low, first, swap(second)).astype(BF16).reshape(8, 16, 128)
    usend[8:16, 0:16] = jnp.where(low, swap(first), second).astype(BF16).reshape(8, 16, 128)
    for t in range(CHIPS):
        usend[t, 16:32] = xs[2, t % 8, c]
    for d in by_distance:
        target = peer(d)
        remote(usend.at[target], ug.at[p], u_ssem, u_rsem, (2 * target + c, z)).start()
    own_u = pltpu.make_async_copy(usend.at[p], ug.at[p], mine_sem.at[2])
    own_u.start()

    for a in range(2):
        for i in range(SIDE):
            c_copy(a, i).wait_send()

    def far_sent(part, span, sem):
        for h in range(2):
            wait_bytes(three_far(part, span, h), f_ssem.at[sem, h])

    def near_sent(part, count):
        for h in range(2):
            wait_bytes(three_near(part, pl.ds(0, count), h), l_ssem.at[part, h])

    for t in (1, 2):

        @pl.when(z == t)
        def _():
            near_sent(0, t)
            far_sent(0, pl.ds(0, t), 0)
            for d in range(SIDE):
                for h in range(2):
                    chain_near(t, h, d).wait_send()

    @pl.when(z > 2)
    def _():
        near_sent(0, 3)
        far_sent(0, pl.ds(0, 3), 0)

    @pl.when(z == 0)
    def _():
        far_sent(0, pl.ds(0, 1), 0)
        far_sent(0, pl.ds(1, 2), 2)

    near_sent(1, 3)
    far_sent(1, pl.ds(0, 3), 1)
    pl.when(z <= 2)(lambda: wait_bytes(rsrecv.at[pl.ds(1, CHIPS - 1)], rs_ssem.at[0, 0]))
    pl.when(z > 2)(lambda: rs_sent(0))
    rs_sent(1)
    for k in range(3):
        sib_copy(k).wait_send()
        if k < 2:
            wait_bytes(xg.at[k, pl.ds(0, CHIPS - 1)], x_ssem.at[k])
            wait_bytes(xg.at[k, pl.ds(0, CHIPS - 1)], x_rsem.at[k])
            own_x(k).wait()

        @pl.when(z == 0)
        def _():
            for d in range(1, PLANES):
                z_copy(k, d).wait_send()

    wait_bytes(ug.at[pl.ds(0, CHIPS - 1)], u_ssem)
    own_u.wait()
    wait_bytes(ug.at[pl.ds(0, CHIPS - 1)], u_rsem)


def assemble(ug, xg, upd, sol):
    low = lanes_low((16, 128))
    early = lax.axis_index("row") < CHIPS
    for t in range(8):
        columns = slice(128 * t, 128 * t + 128)
        even, odd = ug[2 * t, 0:16].astype(F32), ug[2 * t + 1, 0:16].astype(F32)
        upd[:, 0, columns] = jnp.where(low, even, swap(odd))
        upd[:, 1, columns] = jnp.where(low, swap(even), odd)
        for k in range(3):
            even = ug[2 * t, 16:32] if k == 2 else xg[k, 2 * t]
            odd = ug[2 * t + 1, 16:32] if k == 2 else xg[k, 2 * t + 1]
            even, odd = even.astype(F32), odd.astype(F32)
            value = jnp.where(early, jnp.where(low, even, swap(odd)), jnp.where(low, swap(even), odd))
            sol[k, :, columns] = value.astype(BF16)


def per_device(lower_earlier, lower_current, inverse_diagonal, solved_earlier, statistics):
    dma = pltpu.SemaphoreType.DMA
    any_space = pl.BlockSpec(memory_space=pl.ANY)
    vmem = pl.BlockSpec(memory_space=pltpu.VMEM)
    pieces, solved = pl.pallas_call(
        kernel,
        out_shape=(
            jax.ShapeDtypeStruct((16, 32, 128), BF16),
            jax.ShapeDtypeStruct((2, 16, 16, 128), BF16),
        ),
        in_specs=[any_space] * 5,
        out_specs=(any_space, any_space),
        scratch_shapes=[
            pltpu.VMEM((1536, 1024), BF16),
            pltpu.VMEM((2, 2, 16, 16, 1536), BF16),
            pltpu.VMEM((3, 512, 512), BF16),
            pltpu.VMEM((16, 2, 1024), F32),
            pltpu.VMEM((2, 4, 256, 256), BF16),
            pltpu.VMEM((2, 4, 256, 256), BF16),
            pltpu.VMEM((4, 256, 256), F32),
            pltpu.VMEM((2, 4, 4, 128, 128), BF16),
            pltpu.VMEM((16, 128, 128), BF16),
            pltpu.VMEM((2, 2, 4, 4, 64, 128), BF16),
            pltpu.VMEM((2, 2, 4, 64, 128), BF16),
            pltpu.VMEM((2, 2, 4, 4, 3, 16, 256), BF16),
            pltpu.VMEM((3, 128, 128), F32),
            pltpu.VMEM((3, 2, 8, 16, 128), BF16),
            pltpu.VMEM((3, 8, 2, 16, 128), BF16),
            pltpu.VMEM((16, 32, 128), BF16),
            pltpu.VMEM((2, 128, 128), F32),
            dma((2, 2, 3)),
            dma((6,)),
            dma((3,)),
            dma((2, 2)),
            dma((2, 4)), dma((2, 4)),
            dma((2, 2)), dma((2, 2)),
            dma((2, 2)), dma((2, 2)),
            dma((3, 2)), dma((3, 2)),
            dma((2, 4)), dma((2, 2)),
            pltpu.SemaphoreType.REGULAR,
            dma((2, 2)), dma((2, 2)),
            dma, dma((2,)),
            dma((3, 7)), dma((3,)),
            dma((3,)), dma((3,)),
            dma((2,)), dma((2,)),
            dma, dma,
        ],
        compiler_params=pltpu.CompilerParams(
            collective_id=0, has_side_effects=True, vmem_limit_bytes=56 * 1024 * 1024
        ),
        cost_estimate=pl.CostEstimate(flops=3400000000, bytes_accessed=9000000, transcendentals=0),
    )(
        lower_earlier.reshape(2, 3, 16, 2, 16, 512),
        solved_earlier.reshape(1536, 1024),
        lower_current,
        inverse_diagonal,
        statistics,
    )
    return pl.pallas_call(
        assemble,
        out_shape=(
            jax.ShapeDtypeStruct((16, 2, 1024), F32),
            jax.ShapeDtypeStruct((3, 16, 1024), BF16),
        ),
        in_specs=[vmem, vmem],
        out_specs=(vmem, vmem),
        cost_estimate=pl.CostEstimate(flops=200000, bytes_accessed=500000, transcendentals=0),
    )(pieces, solved)


def solution(mesh):
    placed = (
        P("col", "row", None, None),
        P("col", None, "row", None),
        P(),
        P("row", None, None),
        P("row", "col", None),
    )
    return jax.shard_map(
        per_device,
        mesh=mesh,
        in_specs=placed,
        out_specs=(P("row", "col", None), P(None, "row", None)),
        check_vma=False,
    )
```

```python
import jax
import jax.numpy as jnp
from jax import lax
from jax.experimental import pallas as pl
from jax.experimental.pallas import tpu as pltpu
from jax.sharding import PartitionSpec as P

MESH = pl.DeviceIdType.MESH
F32 = jnp.float32
BF16 = jnp.bfloat16
SIDE = 4
CHIPS = 16
PLANES = 8


def lanes_low(shape):
    return lax.broadcasted_iota(jnp.int32, shape, len(shape) - 1) < 64


def swap(value):
    return pltpu.roll(value, 64, 1)


def dot(a, b):
    return jnp.dot(a, b, preferred_element_type=F32)


def wait_bytes(ref, sem):
    pltpu.make_async_copy(ref, ref, sem).wait()


def kernel(
    le, s, lc, inv, stat, ug, xg,
    sv, lev, invv, statv, csend, crecv, acc, rssend, rsrecv, mid, last, lg, q, xs, usend, red,
    le_sem, load_sem, mine_sem, own_sem, c_ssem, c_rsem, rs_ssem, rs_rsem, l_ssem, l_rsem, f_ssem, f_rsem, ready_sem,
    r2_ssem, r2_rsem, z_ssem, z_rsem, q_ssem, q_rsem, x_ssem, x_rsem, u_ssem, u_rsem,
):
    row = lax.axis_index("row")
    z = lax.axis_index("col")
    c = lax.rem(row, 2)
    p = row // 2
    x = p // SIDE
    y = lax.rem(p, SIDE)
    sib = (row + 1 - 2 * c, z)
    low = lanes_low((128, 128))
    steps = (0, 1, 2, 1)
    by_distance = sorted(range(1, CHIPS), key=lambda d: -steps[d // SIDE] - steps[d % SIDE])

    def peer(d):
        px = lax.rem(x + d // SIDE, SIDE)
        py = lax.rem(y + lax.rem(d, SIDE), SIDE)
        return px * SIDE + py

    def x_peer(d):
        return 2 * (lax.rem(x + d, SIDE) * SIDE + y) + c

    def y_peer(d):
        return 2 * (x * SIDE + lax.rem(y + d, SIDE)) + c

    def remote(src, dst, ssem, rsem, device):
        return pltpu.make_async_remote_copy(
            src_ref=src, dst_ref=dst, send_sem=ssem, recv_sem=rsem, device_id=device, device_id_type=MESH
        )

    def block_columns(i):
        return pl.ds(pl.multiple_of(lax.rem(x + i, SIDE) * 256, 256), 256)

    def nth(t):
        return lax.rem(t + 2, SIDE)

    def le_load(a, slot, b):
        half = c if slot else 1 - c
        return pltpu.make_async_copy(
            le.at[a, b, :, half], lev.at[a, slot, :, :, pl.ds(512 * b, 512)], le_sem.at[a, slot, b]
        )

    def s_load(t):
        columns = block_columns(nth(t))
        return pltpu.make_async_copy(s.at[:, columns], sv.at[:, columns], load_sem.at[t])

    def le_loads(a):
        return [le_load(a, slot, b) for slot in range(2) for b in range(3)]

    inv_load = pltpu.make_async_copy(inv, invv, load_sem.at[4])
    stat_load = pltpu.make_async_copy(stat, statv, load_sem.at[5])
    for cp in le_loads(0) + [s_load(t) for t in range(SIDE)] + le_loads(1) + [stat_load, inv_load]:
        cp.start()

    barrier = pltpu.get_barrier_semaphore()

    def greet(d, carry):
        pl.semaphore_signal(barrier, inc=1, device_id=(2 * peer(d) + c, z), device_id_type=MESH)
        return carry

    def signal(sem, device):
        pl.semaphore_signal(sem, inc=1, device_id=device, device_id_type=MESH)

    @pl.when(z <= 2)
    def _():
        for d in (4, 3, 5, 6, 7, 2, 1):
            signal(barrier, (row, lax.rem(z + d, PLANES)))

    lax.fori_loop(1, CHIPS, greet, 0)
    signal(barrier, sib)
    partners = CHIPS + jnp.where(z <= 2, 2, 3)

    def c_copy(a, i):
        return remote(csend.at[a, i], crecv.at[a, i], c_ssem.at[a, i], c_rsem.at[a, i], sib)

    def multiply(a, t):
        if a == 0:
            s_load(t).wait()
        both = dot(lev[a].reshape(512, 1536), sv[:, block_columns(nth(t))])
        csend[a, t] = both[0:256].astype(BF16)
        acc[t] = both[256:512]

    def rs_send(a, i, j):
        py = lax.rem(y + j, SIDE)
        px = lax.rem(x + i, SIDE)
        remote(
            rssend.at[a, i, py],
            rsrecv.at[SIDE * i + j],
            rs_ssem.at[a, 0],
            rs_rsem.at[a, 0],
            (2 * (px * SIDE + py) + c, z),
        ).start()

    top, bottom = pl.ds(0, 64), pl.ds(64, 64)

    def first_x(a, i):
        remote(
            rssend.at[a, i, :, top],
            mid.at[a, 0, i],
            rs_ssem.at[a, 0],
            rs_rsem.at[a, 0],
            (2 * (lax.rem(x + i, SIDE) * SIDE + y) + c, z),
        ).start()

    def first_y(a):
        for j in (2, 1, 3):
            remote(
                rssend.at[a, :, lax.rem(y + j, SIDE), bottom],
                mid.at[a, 1, j],
                rs_ssem.at[a, 1],
                rs_rsem.at[a, 1],
                (y_peer(j), z),
            ).start()

    def rs_relay(a):
        wait_bytes(mid.at[a, 0, pl.ds(1, 3)], rs_rsem.at[a, 0])
        total = rssend[a, 0, :, 0:64].astype(F32)
        for d in range(1, SIDE):
            total = total + mid[a, 0, d].astype(F32)
        mid[a, 0, 0] = total.astype(BF16)
        for j in (2, 1, 3):
            remote(
                mid.at[a, 0, 0, lax.rem(y + j, SIDE)], last.at[a, 0, j], r2_ssem.at[a, 0], r2_rsem.at[a, 0], (y_peer(j), z)
            ).start()
        wait_bytes(mid.at[a, 1, pl.ds(1, 3)], rs_rsem.at[a, 1])
        total = rssend[a, :, y, 64:128].astype(F32)
        for d in range(1, SIDE):
            total = total + mid[a, 1, d].astype(F32)
        mid[a, 1, 0] = total.astype(BF16)
        for i in (2, 1, 3):
            remote(
                mid.at[a, 1, 0, i], last.at[a, 1, i], r2_ssem.at[a, 1], r2_rsem.at[a, 1], (x_peer(i), z)
            ).start()

    def rs_last(a):
        for h in range(2):
            wait_bytes(last.at[a, h, pl.ds(1, 3)], r2_rsem.at[a, h])
            total = mid[a, h, 0, (0 if h else y)].astype(F32)
            for d in range(1, SIDE):
                total = total + last[a, h, d].astype(F32)
            red[a, 64 * h : 64 * h + 64] = -total

    def rs_sent(a):
        for h in range(2):
            wait_bytes(mid.at[a, h, pl.ds(1, 3)], rs_ssem.at[a, h])
            wait_bytes(last.at[a, h, pl.ds(1, 3)], r2_ssem.at[a, h])

    def finish(a, turn):
        i = nth(turn)
        columns = block_columns(i)
        c_copy(a, turn).wait_recv()
        acc[turn] = acc[turn] + crecv[a, turn].astype(F32)
        mine = pl.ds(pl.multiple_of(16 * p, 16), 16)
        acc[turn, mine, :] = acc[turn, mine, :] - statv[:, a, columns]
        for t in range(2):
            lo = acc[turn, 0:128, 128 * t : 128 * t + 128]
            hi = acc[turn, 128:256, 128 * t : 128 * t + 128]
            rssend[a, i, 2 * t] = jnp.where(low, lo, swap(hi)).astype(BF16)
            rssend[a, i, 2 * t + 1] = jnp.where(low, swap(lo), hi).astype(BF16)

        def sends():
            for j in (2, 1, 3):
                rs_send(a, i, j)
            pl.when(i > 0)(lambda: rs_send(a, i, 0))

        if a == 0:
            pl.when(z <= 2)(sends)
            pl.when((z > 2) & (i > 0))(lambda: first_x(a, i))
        else:
            pl.when(i > 0)(lambda: first_x(a, i))

    def turns(a, first, last_turn):
        def turn(t, carry):
            @pl.when(t < SIDE)
            def _():
                multiply(a, t)
                c_copy(a, t).start()

            pl.when(t >= 2)(lambda: finish(a, t - 2))
            return carry

        lax.fori_loop(first, last_turn, turn, 0)

    for cp in le_loads(0):
        cp.wait()
    multiply(0, 0)
    pl.semaphore_wait(barrier, partners)
    c_copy(0, 0).start()

    @pl.when(z > 2)
    def _():
        for t in range(3):
            signal(ready_sem, (row, t))

    halves = (pl.ds(0, 256), pl.ds(256, 256))

    def along(h, d):
        return y_peer(d) if h else x_peer(d)

    def own_slot(part, h, span):
        return lg.at[part, 1, x, y, span] if h else lg.at[part, 0, y, x, span]

    def near(part, count):
        for d in (2, 1, 3):
            for h in range(2):
                remote(
                    lc.at[part, pl.ds(0, count), :, halves[h]],
                    own_slot(part, h, pl.ds(0, count)),
                    l_ssem.at[part, h],
                    l_rsem.at[part, h],
                    (along(h, d), z),
                ).start()

    own_part = [
        [
            pltpu.make_async_copy(lc.at[t, :, :, halves[h]], own_slot(t, h, pl.ds(0, 3)), own_sem.at[t, h])
            for h in range(2)
        ]
        for t in range(2)
    ]

    def own_start(part):
        for cp in own_part[part]:
            cp.start()

    for t in (1, 2):
        pl.when(z == t)(lambda: near(0, t))
    pl.when(z > 2)(lambda: near(0, 3))
    pl.when(z > 0)(lambda: own_start(0))
    near(1, 3)
    own_start(1)

    stat_load.wait()
    turns(0, 1, SIDE + 2)
    pl.when(z > 2)(lambda: first_y(0))

    def source(part, span, h):
        return lg.at[part, 1, x, :, span] if h else lg.at[part, 0, y, :, span]

    def far(part, span, sem):
        for h in range(2):
            for d in (2, 1, 3):
                device = (along(1 - h, d), z)
                remote(
                    source(part, span, h), source(part, span, h), f_ssem.at[sem, h], f_rsem.at[sem, h], device
                ).start()

    def three_near(part, span, h):
        return lg.at[part, h, 0, pl.ds(0, 3), span]

    def three_far(part, span, h):
        return lg.at[part, h, pl.ds(0, 3), :, span]

    def relay(part, count):
        for cp in own_part[part]:
            cp.wait()
        for h in range(2):
            wait_bytes(three_near(part, pl.ds(0, count), h), l_rsem.at[part, h])
        far(part, pl.ds(0, count), part)

    def gather_wait(part, span, sem):
        for h in range(2):
            wait_bytes(three_far(part, span, h), f_rsem.at[sem, h])

    for t in (1, 2):
        pl.when(z == t)(lambda: relay(0, t))

    def between():
        @pl.when(z > 2)
        def _():
            relay(0, 3)
            relay(1, 3)

    for cp in le_loads(1):
        cp.wait()
    turns(1, 0, 3)
    between()
    turns(1, 3, SIDE + 2)
    first_y(1)
    inv_load.wait()

    @pl.when(z <= 2)
    def _():
        wait_bytes(rsrecv.at[pl.ds(1, CHIPS - 1)], rs_rsem.at[0, 0])
        total = rssend[0, 0, y].astype(F32)
        for d in range(1, CHIPS):
            total = total + rsrecv[d].astype(F32)
        red[0] = -total

    @pl.when(z > 2)
    def _():
        rs_relay(0)
        rs_relay(1)
        rs_last(0)

    @pl.when((z == 1) | (z == 2))
    def _():
        relay(1, 3)
        rs_relay(1)

    def applied(block, k):
        part, slot = divmod(block, 3)
        solved = xs[k].reshape(256, 128)
        chips = [(i, j) for i in range(SIDE) for j in range(SIDE)]
        first = dot(jnp.concatenate([lg[part, 0, j, i, slot] for i, j in chips], axis=0), solved)
        second = dot(jnp.concatenate([lg[part, 1, i, j, slot] for i, j in chips], axis=0), solved)
        return jnp.where(low, first[0:128], second[128:256]) + swap(
            jnp.where(low, first[128:256], second[0:128])
        )

    def update(part, k):
        red[part] = red[part] - applied(3 * part + k, k)

    def a1_ready():
        gather_wait(1, pl.ds(0, 3), 1)
        rs_last(1)

    def own_x(k):
        return pltpu.make_async_copy(xs.at[k, lax.rem(p, 8), c], xg.at[k, p], mine_sem.at[k])

    def x_send(k):
        def send(d, carry):
            target = peer(d)
            remote(
                xs.at[k, lax.rem(target, 8), c], xg.at[k, p], x_ssem.at[k], x_rsem.at[k], (2 * target + c, z)
            ).start()
            return carry

        lax.fori_loop(1, CHIPS, send, 0)
        own_x(k).start()

    def z_copy(k, d):
        return remote(
            q.at[k, c], q.at[k, c], z_ssem.at[k, d - 1], z_rsem.at[k], (row, lax.rem(z + d, PLANES))
        )

    def sib_copy(k):
        return remote(q.at[k, c], q.at[k, c], q_ssem.at[k], q_rsem.at[k], sib)

    def sib_back(k):
        return remote(q.at[k, 1 - c], q.at[k, 1 - c], q_ssem.at[k], q_rsem.at[k], sib)

    orders = ((1, 2, 4, 5, 3, 6, 7), (1, 4, 5, 3, 6, 2, 7), (6, 3, 7, 2, 5, 1, 4))
    for k in range(3):

        @pl.when(z == k)
        def _():
            q[k, c] = red[0].astype(BF16).reshape(8, 16, 128)
            sib_copy(k).start()
            pl.semaphore_wait(ready_sem, PLANES - 3)
            for d in orders[k]:
                z_copy(k, d).start()
            if k == 0:
                relay(1, 3)
                rs_relay(1)

        @pl.when(z != k)
        def _():
            if k > 0:
                pl.when((z == 0) | (z > 2))(lambda: x_send(k - 1))
            if k == 2:

                @pl.when(z == 1)
                def _():
                    x_send(0)
                    x_send(1)

            z_copy(k, 1).wait_recv()
            sib_copy(k).start()
            if k == 2:

                @pl.when(z != 2)
                def _():
                    pl.when(z > 2)(lambda: gather_wait(0, pl.ds(0, 3), 0))
                    a1_ready()
                    for j in range(2):
                        update(1, j)
                        pl.when(z > 2)(lambda: update(0, j))


        sib_back(k).wait_recv()
        pivotal = jnp.concatenate([q[k, h, g] for g in range(8) for h in range(2)], axis=0)
        left = dot(invv[k, :, 0:256], pivotal)
        right = dot(invv[k, 256:512, 256:512], pivotal)
        low_x = lanes_low((256, 128))
        solved = jnp.where(low_x, left[0:256], right + swap(left[256:512]))
        xs[k] = solved.astype(BF16).reshape(8, 2, 16, 128)

        if k == 0:
            for t in (1, 2):

                @pl.when(z == t)
                def _():
                    gather_wait(0, pl.ds(0, t), 0)
                    update(0, 0)

        if k == 1:
            pl.when(z == 2)(lambda: update(0, 1))

    @pl.when(z == 2)
    def _():
        a1_ready()
        for j in range(2):
            x_send(j)
            update(1, j)

    update(1, 2)
    pl.when(z > 2)(lambda: update(0, 2))
    first, second = red[0], red[1]
    usend[0:8, 0:16] = jnp.where(low, first, swap(second)).astype(BF16).reshape(8, 16, 128)
    usend[8:16, 0:16] = jnp.where(low, swap(first), second).astype(BF16).reshape(8, 16, 128)
    for t in range(CHIPS):
        usend[t, 16:32] = xs[2, t % 8, c]
    for d in by_distance:
        target = peer(d)
        remote(usend.at[target], ug.at[p], u_ssem, u_rsem, (2 * target + c, z)).start()
    own_u = pltpu.make_async_copy(usend.at[p], ug.at[p], mine_sem.at[2])
    own_u.start()

    for a in range(2):
        for i in range(SIDE):
            c_copy(a, i).wait_send()

    def far_sent(part, span, sem):
        for h in range(2):
            wait_bytes(three_far(part, span, h), f_ssem.at[sem, h])

    def near_sent(part, count):
        for h in range(2):
            wait_bytes(three_near(part, pl.ds(0, count), h), l_ssem.at[part, h])

    for t in (1, 2):

        @pl.when(z == t)
        def _():
            near_sent(0, t)
            far_sent(0, pl.ds(0, t), 0)

    @pl.when(z > 2)
    def _():
        near_sent(0, 3)
        far_sent(0, pl.ds(0, 3), 0)

    near_sent(1, 3)
    far_sent(1, pl.ds(0, 3), 1)
    pl.when(z <= 2)(lambda: wait_bytes(rsrecv.at[pl.ds(1, CHIPS - 1)], rs_ssem.at[0, 0]))
    pl.when(z > 2)(lambda: rs_sent(0))
    rs_sent(1)
    for k in range(3):
        sib_copy(k).wait_send()
        if k < 2:
            wait_bytes(xg.at[k, pl.ds(0, CHIPS - 1)], x_ssem.at[k])
            wait_bytes(xg.at[k, pl.ds(0, CHIPS - 1)], x_rsem.at[k])
            own_x(k).wait()

        @pl.when(z == k)
        def _():
            for d in range(1, PLANES):
                z_copy(k, d).wait_send()

    wait_bytes(ug.at[pl.ds(0, CHIPS - 1)], u_ssem)
    own_u.wait()
    wait_bytes(ug.at[pl.ds(0, CHIPS - 1)], u_rsem)


def assemble(ug, xg, upd, sol):
    low = lanes_low((16, 128))
    early = lax.axis_index("row") < CHIPS
    for t in range(8):
        columns = slice(128 * t, 128 * t + 128)
        even, odd = ug[2 * t, 0:16].astype(F32), ug[2 * t + 1, 0:16].astype(F32)
        upd[:, 0, columns] = jnp.where(low, even, swap(odd))
        upd[:, 1, columns] = jnp.where(low, swap(even), odd)
        for k in range(3):
            even = ug[2 * t, 16:32] if k == 2 else xg[k, 2 * t]
            odd = ug[2 * t + 1, 16:32] if k == 2 else xg[k, 2 * t + 1]
            even, odd = even.astype(F32), odd.astype(F32)
            value = jnp.where(early, jnp.where(low, even, swap(odd)), jnp.where(low, swap(even), odd))
            sol[k, :, columns] = value.astype(BF16)


def per_device(lower_earlier, lower_current, inverse_diagonal, solved_earlier, statistics):
    dma = pltpu.SemaphoreType.DMA
    any_space = pl.BlockSpec(memory_space=pl.ANY)
    vmem = pl.BlockSpec(memory_space=pltpu.VMEM)
    pieces, solved = pl.pallas_call(
        kernel,
        out_shape=(
            jax.ShapeDtypeStruct((16, 32, 128), BF16),
            jax.ShapeDtypeStruct((2, 16, 16, 128), BF16),
        ),
        in_specs=[any_space] * 5,
        out_specs=(any_space, any_space),
        scratch_shapes=[
            pltpu.VMEM((1536, 1024), BF16),
            pltpu.VMEM((2, 2, 16, 16, 1536), BF16),
            pltpu.VMEM((3, 512, 512), BF16),
            pltpu.VMEM((16, 2, 1024), F32),
            pltpu.VMEM((2, 4, 256, 256), BF16),
            pltpu.VMEM((2, 4, 256, 256), BF16),
            pltpu.VMEM((4, 256, 256), F32),
            pltpu.VMEM((2, 4, 4, 128, 128), BF16),
            pltpu.VMEM((16, 128, 128), BF16),
            pltpu.VMEM((2, 2, 4, 4, 64, 128), BF16),
            pltpu.VMEM((2, 2, 4, 64, 128), BF16),
            pltpu.VMEM((2, 2, 4, 4, 3, 16, 256), BF16),
            pltpu.VMEM((3, 2, 8, 16, 128), BF16),
            pltpu.VMEM((3, 8, 2, 16, 128), BF16),
            pltpu.VMEM((16, 32, 128), BF16),
            pltpu.VMEM((2, 128, 128), F32),
            dma((2, 2, 3)),
            dma((6,)),
            dma((3,)),
            dma((2, 2)),
            dma((2, 4)), dma((2, 4)),
            dma((2, 2)), dma((2, 2)),
            dma((2, 2)), dma((2, 2)),
            dma((2, 2)), dma((2, 2)),
            pltpu.SemaphoreType.REGULAR,
            dma((2, 2)), dma((2, 2)),
            dma((3, 7)), dma((3,)),
            dma((3,)), dma((3,)),
            dma((2,)), dma((2,)),
            dma, dma,
        ],
        compiler_params=pltpu.CompilerParams(
            collective_id=0, has_side_effects=True, vmem_limit_bytes=56 * 1024 * 1024
        ),
        cost_estimate=pl.CostEstimate(flops=3400000000, bytes_accessed=9000000, transcendentals=0),
    )(
        lower_earlier.reshape(2, 3, 16, 2, 16, 512),
        solved_earlier.reshape(1536, 1024),
        lower_current,
        inverse_diagonal,
        statistics,
    )
    return pl.pallas_call(
        assemble,
        out_shape=(
            jax.ShapeDtypeStruct((16, 2, 1024), F32),
            jax.ShapeDtypeStruct((3, 16, 1024), BF16),
        ),
        in_specs=[vmem, vmem],
        out_specs=(vmem, vmem),
        cost_estimate=pl.CostEstimate(flops=200000, bytes_accessed=500000, transcendentals=0),
    )(pieces, solved)


def solution(mesh):
    placed = (
        P("col", "row", None, None),
        P("col", None, "row", None),
        P(),
        P("row", None, None),
        P("row", "col", None),
    )
    return jax.shard_map(
        per_device,
        mesh=mesh,
        in_specs=placed,
        out_specs=(P("row", "col", None), P(None, "row", None)),
        check_vma=False,
    )
```
